128 devices in a mesh: frame: 8 (over z, y_lo), tile: 16 (over x, y_hi, core).
Axes of the slice: x: 4, y: 4 (y_hi: 2, y_lo: 2; y = y_hi * 2 + y_lo), z: 4, core: 2. Of those that a mesh axis runs over, the one named last changes fastest.
Arguments:
- patch_tokens: bfloat16 [32, 1024, 768], P('frame', 'tile'), may hold values from -6 to 6
- gain_time: float32 [768], replicated, may hold values from 0.1 to 1.9
- qkv_time: bfloat16 [768, 2304], replicated, may hold values from -1 to 1
- out_time: bfloat16 [768, 768], replicated, may hold values from -0.21875 to 0.21875
- gain_space: float32 [768], replicated, may hold values from 0.1 to 1.9
- qkv_space: bfloat16 [768, 2304], replicated, may hold values from -1 to 1
- out_space: bfloat16 [768, 768], replicated, may hold values from -0.21875 to 0.21875
- cotangent: bfloat16 [32, 1024, 768], P('frame', 'tile'), may hold values from -6 to 6
Outputs:
- block_output: bfloat16 [32, 1024, 768], P('frame', 'tile')
- input_grad: bfloat16 [32, 1024, 768], P('frame', 'tile')
The draws below stay inside these ranges and needn't reach their ends.
All inputs are finite; a program needn't handle non-finite values.
Results may differ from the reference program's by a relative error of at most 0.028.
Values may be sent and summed in bfloat16 or wider, within the bound.
No kernel may reach another device: no remote copies, remote signals or barrier semaphores. Data moves between devices by JAX's collectives and lax.ppermute only.
A program may use at most 192 MiB of HBM per device.

```python
import math
import jax
import jax.numpy as jnp
from jax import lax

D = 768
HEADS = 12
PATCHES = 1024
FRAMES = 32
N_TILE = 16


def qkv_weight(key, spread_max):
    key_base, key_scale = jax.random.split(key)
    base_draw = jnp.clip(jax.random.normal(key_base, (D, 3 * D), jnp.float32), -3.5, 3.5) * D ** (-0.5)
    head_scale = jnp.exp(jax.random.uniform(key_scale, (HEADS,), jnp.float32, 0.0, math.log(spread_max)))
    column_scale = jnp.repeat(head_scale, D // HEADS)
    query_cols = base_draw[:, :D] * column_scale
    key_cols = base_draw[:, D:2 * D] * column_scale
    joined = jnp.concatenate([query_cols, key_cols, base_draw[:, 2 * D:]], axis=1)
    return jnp.clip(joined, -1.0, 1.0).astype(jnp.bfloat16)


def draw_qkv_time(key, part):
    key = jax.random.fold_in(key, 11)
    return qkv_weight(key, 1.0)


def draw_qkv_space(key, part):
    key = jax.random.fold_in(key, 23)
    return qkv_weight(key, 1.0)


def steps_of(stream_key, shape, shards, smallest, top_value):
    factor_of, own = 1.0, jax.random.fold_in(stream_key, 6)
    for dim, blocks in shards:
        steps = jnp.exp(jax.random.uniform(jax.random.fold_in(own, dim), (blocks,), jnp.float32, smallest / len(shards), top_value / len(shards)))
        factor_of = factor_of * jnp.repeat(steps, shape[dim] // blocks).reshape([-1 if axis == dim else 1 for axis in range(len(shape))])
    return factor_of


def normal_values(stream_key, extent, width, limit, cuts=(), kind=jnp.bfloat16):
    values = jax.random.normal(stream_key, extent, jnp.float32) * width
    if len(cuts) > 0:
        values = steps_of(stream_key, extent, cuts, -0.22, 0.18) * values
    return jnp.clip(values, min=-limit, max=limit).astype(kind)


def setup_inputs(seed: int = 0) -> dict:
    splits = jax.random.split(jax.random.key(seed), 9)
    return {
        "patch_tokens": normal_values(splits[0], (FRAMES, PATCHES, D), 1.0, 6.0, ((0, 8), (1, 16))),
        "gain_time": jnp.clip(1.0 + 0.18 * jax.random.normal(splits[1], (D,), jnp.float32), 0.1, 1.9),
        "qkv_time": draw_qkv_time(jax.random.fold_in(splits[8], 71), 0),
        "out_time": normal_values(splits[3], (D, D), D ** -0.5, 0.21875),
        "gain_space": jnp.clip(1.0 + 0.18 * jax.random.normal(splits[4], (D,), jnp.float32), 0.1, 1.9),
        "qkv_space": draw_qkv_space(jax.random.fold_in(splits[8], 71), 0),
        "out_space": normal_values(splits[6], (D, D), D ** -0.5, 0.21875),
        "cotangent": normal_values(splits[7], (FRAMES, PATCHES, D), 1.0, 6.0, ((0, 8), (1, 16))),
    }


EPSILON = 1e-05

def round_half(array):
    return lax.optimization_barrier(array.astype(jnp.bfloat16)).astype(jnp.float32)

def split_heads(array):
    return array.reshape(array.shape[:-1] + (HEADS, array.shape[-1] // HEADS))

def join_heads(array):
    return array.reshape(array.shape[:-2] + (array.shape[-2] * array.shape[-1],))

def norm_forward(tokens_in, gain):
    wide = tokens_in.astype(jnp.float32)
    average = lax.optimization_barrier(jnp.mean(wide, axis=-1, keepdims=True))
    centred = wide - average
    inverse = lax.rsqrt(lax.optimization_barrier(jnp.mean(centred * centred, axis=-1, keepdims=True)) + EPSILON)
    normed = centred * inverse
    return ((normed * gain).astype(jnp.bfloat16), normed, inverse)

def norm_backward(grad_normed, gain, normed, inverse):
    scaled = grad_normed * gain
    return inverse * (scaled - lax.optimization_barrier(jnp.mean(scaled, axis=-1, keepdims=True)) - normed * lax.optimization_barrier(jnp.mean(scaled * normed, axis=-1, keepdims=True)))

def probabilities(queries, key_rows, query_form, key_form):
    scores = jnp.einsum(query_form + ',' + key_form + '->ahij', queries.astype(jnp.float32), key_rows.astype(jnp.float32)) * queries.shape[-1] ** (-0.5)
    row_max = lax.optimization_barrier(jnp.max(scores, axis=-1, keepdims=True))
    lifted = jnp.exp(scores - row_max)
    return lifted / lax.optimization_barrier(jnp.sum(lifted, axis=-1, keepdims=True))

def attend(queries, key_rows, value_rows, query_form, key_form):
    weights = round_half(probabilities(queries, key_rows, query_form, key_form))
    return jnp.einsum('ahij,' + key_form + '->' + query_form, weights, value_rows.astype(jnp.float32)).astype(jnp.bfloat16)

def grad_pieces(grad_out, queries, key_rows, value_rows, attended, query_form, key_form):
    weights = probabilities(queries, key_rows, query_form, key_form)
    grad_weights = jnp.einsum(query_form + ',' + key_form + '->ahij', grad_out.astype(jnp.float32), value_rows.astype(jnp.float32))
    delta_rows = jnp.einsum(query_form + ',' + query_form + '->ahi', grad_out.astype(jnp.float32), attended.astype(jnp.float32))
    grad_scores = round_half(weights * (grad_weights - delta_rows[..., None]) * queries.shape[-1] ** (-0.5))
    grad_query = jnp.einsum('ahij,' + key_form + '->' + query_form, grad_scores, key_rows.astype(jnp.float32))
    return (grad_query, grad_scores, round_half(weights))

def time_attend(queries, key_rows, value_rows):
    return attend(queries, key_rows, value_rows, 'iahe', 'jahe')

def space_frame(frame_items):
    query_frame, key_frame, value_frame = frame_items
    return attend(query_frame[None], key_frame[None], value_frame[None], 'aihe', 'ajhe')[0]

def space_attend(queries, key_rows, value_rows):
    return lax.map(space_frame, (queries, key_rows, value_rows))

def time_grads(grad_out, queries, key_rows, value_rows, attended):
    grad_query, grad_scores, weights_half = grad_pieces(grad_out, queries, key_rows, value_rows, attended, 'iahe', 'jahe')
    grad_key = jnp.einsum('ahij,iahe->jahe', grad_scores, queries.astype(jnp.float32))
    grad_value = jnp.einsum('ahij,iahe->jahe', weights_half, grad_out.astype(jnp.float32))
    return (grad_query, grad_key, grad_value)

def space_frame_grads(frame_items):
    grad_frame, query_frame, key_frame, value_frame, output_frame = frame_items
    grad_query, grad_scores, weights_half = grad_pieces(grad_frame[None], query_frame[None], key_frame[None], value_frame[None], output_frame[None], 'aihe', 'ajhe')
    patch_count = query_frame.shape[0]
    block_rows = patch_count // N_TILE
    score_blocks = grad_scores[0].reshape(HEADS, N_TILE, block_rows, patch_count)
    weight_blocks = weights_half[0].reshape(HEADS, N_TILE, block_rows, patch_count)
    query_blocks = query_frame.astype(jnp.float32).reshape(N_TILE, block_rows, HEADS, -1)
    grad_blocks = grad_frame.astype(jnp.float32).reshape(N_TILE, block_rows, HEADS, -1)
    grad_key = lax.optimization_barrier(jnp.sum(round_half(jnp.einsum('hbij,bihe->bjhe', score_blocks, query_blocks)), axis=0))
    grad_value = lax.optimization_barrier(jnp.sum(round_half(jnp.einsum('hbij,bihe->bjhe', weight_blocks, grad_blocks)), axis=0))
    return (grad_query[0], grad_key, grad_value)

def space_grads(grad_out, queries, key_rows, value_rows, attended):
    return lax.map(space_frame_grads, (grad_out, queries, key_rows, value_rows, attended))

def sublayer_forward(tokens_in, gain, weight_qkv, weight_out, attend_fn):
    normed_half, normed, inverse = norm_forward(tokens_in, gain)
    projected = jnp.dot(normed_half, weight_qkv, preferred_element_type=jnp.float32).astype(jnp.bfloat16)
    features = tokens_in.shape[-1]
    queries = split_heads(projected[..., :features])
    key_rows = split_heads(projected[..., features:2 * features])
    value_rows = split_heads(projected[..., 2 * features:])
    attended = attend_fn(queries, key_rows, value_rows)
    mixed = tokens_in.astype(jnp.float32) + jnp.dot(join_heads(attended), weight_out, preferred_element_type=jnp.float32)
    return (mixed.astype(jnp.bfloat16), (normed, inverse, queries, key_rows, value_rows, attended))

def sublayer_backward(grad_in, gain, weight_qkv, weight_out, cache, grad_fn):
    normed, inverse, queries, key_rows, value_rows, attended = cache
    grad_out = split_heads(jnp.einsum('fpd,ed->fpe', grad_in.astype(jnp.float32), weight_out.astype(jnp.float32)).astype(jnp.bfloat16))
    grad_query, grad_key, grad_value = grad_fn(grad_out, queries, key_rows, value_rows, attended)
    grad_qkv = jnp.concatenate([join_heads(grad_query).astype(jnp.bfloat16), join_heads(grad_key).astype(jnp.bfloat16), join_heads(grad_value).astype(jnp.bfloat16)], axis=-1)
    grad_normed = jnp.einsum('fpc,dc->fpd', grad_qkv.astype(jnp.float32), weight_qkv.astype(jnp.float32))
    return (grad_in.astype(jnp.float32) + norm_backward(grad_normed, gain, normed, inverse)).astype(jnp.bfloat16)

def reference(patch_tokens, gain_time, qkv_time, out_time, gain_space, qkv_space, out_space, cotangent):
    hidden, cache_time = sublayer_forward(patch_tokens, gain_time, qkv_time, out_time, time_attend)
    block_output, cache_space = sublayer_forward(hidden, gain_space, qkv_space, out_space, space_attend)
    grad_hidden = sublayer_backward(cotangent, gain_space, qkv_space, out_space, cache_space, space_grads)
    input_grad = sublayer_backward(grad_hidden, gain_time, qkv_time, out_time, cache_time, time_grads)
    return (block_output, input_grad)
```

```python
import functools

import jax
import jax.numpy as jnp
from jax import lax
from jax.experimental import pallas as pl
from jax.experimental.pallas import tpu as pltpu
from jax.sharding import PartitionSpec as P

HEADS = 12
EPSILON = 1e-05
F32 = jnp.float32
BF16 = jnp.bfloat16
VMEM = pl.BlockSpec(memory_space=pltpu.VMEM)
ANY = pl.BlockSpec(memory_space=pl.ANY)
LIMIT = 56 * 1024 * 1024


def dot(a, b):
    return jnp.dot(a, b, preferred_element_type=F32)


def dot_last(a, b):
    return lax.dot_general(a, b, (((1,), (1,)), ((), ())), preferred_element_type=F32)


def norm_stats(wide):
    average = jnp.mean(wide, axis=-1, keepdims=True)
    centred = wide - average
    inverse = lax.rsqrt(jnp.mean(centred * centred, axis=-1, keepdims=True) + EPSILON)
    return centred * inverse, inverse


def norm_backward(grad_normed, gain, normed, inverse):
    scaled = grad_normed * gain
    return inverse * (
        scaled
        - jnp.mean(scaled, axis=-1, keepdims=True)
        - normed * jnp.mean(scaled * normed, axis=-1, keepdims=True)
    )


def same_patch(tokens, patches):
    rows = lax.broadcasted_iota(jnp.int32, (tokens, tokens), 0)
    columns = lax.broadcasted_iota(jnp.int32, (tokens, tokens), 1)
    return (rows % patches) == (columns % patches)


def time_forward_kernel(
    patches, groups,
    both_ref, gain_time_ref, gain_space_ref, qkv_time_hbm, out_time_hbm, qkv_space_hbm, out_space_hbm,
    send_ref, hidden_ref, qkv_ref, attended_ref, prob_ref,
    qkv_time_ref, out_time_ref, qkv_space_ref, out_space_ref, sems,
):
    copies = [
        pltpu.make_async_copy(src, dst, sems.at[n])
        for n, (src, dst) in enumerate((
            (qkv_time_hbm, qkv_time_ref), (out_space_hbm, out_space_ref),
            (out_time_hbm, out_time_ref), (qkv_space_hbm, qkv_space_ref),
        ))
    ]
    for copy in copies:
        copy.start()
    tokens, features = hidden_ref.shape
    size = features // HEADS
    part = features // groups
    tokens_in = both_ref[:, 0].reshape(tokens, features).astype(F32)
    cotangent = both_ref[:, 1].reshape(tokens, features)
    normed, _ = norm_stats(tokens_in)
    normed_half = (normed * gain_time_ref[...]).astype(BF16)
    copies[0].wait()
    qkv = dot(normed_half, qkv_time_ref[...]).astype(BF16)
    qkv_ref[...] = qkv
    copies[1].wait()
    grad_out = dot_last(cotangent, out_space_ref[...]).astype(BF16)
    qkv_t = qkv.T
    mask = same_patch(tokens, patches)
    outputs = []
    for h in range(HEADS):
        keys = qkv[:, features + h * size : features + (h + 1) * size]
        queries_t = qkv_t[h * size : (h + 1) * size] * jnp.asarray(size ** -0.5, BF16)
        scores = jnp.where(mask, dot(keys, queries_t), -1e30)
        lifted = jnp.exp(scores - jnp.max(scores, axis=0, keepdims=True))
        prob = (lifted / jnp.sum(lifted, axis=0, keepdims=True)).astype(BF16)
        prob_ref[h] = prob
        values_t = qkv_t[2 * features + h * size : 2 * features + (h + 1) * size]
        outputs.append(dot(values_t, prob))
    attended = jnp.concatenate(outputs, axis=0).T.astype(BF16)
    attended_ref[...] = attended
    copies[2].wait()
    hidden = (tokens_in + dot(attended, out_time_ref[...])).astype(BF16)
    hidden_ref[...] = hidden
    normed_space, _ = norm_stats(hidden.astype(F32))
    space_half = (normed_space * gain_space_ref[...]).astype(BF16)
    copies[3].wait()
    space = dot(space_half, qkv_space_ref[...]).astype(BF16)
    for g in range(groups):
        send_ref[g] = jnp.concatenate(
            [space[:, n * features + g * part : n * features + (g + 1) * part] for n in range(3)]
            + [grad_out[:, g * part : (g + 1) * part]],
            axis=1,
        )


def space_kernel(heads, block, got_ref, back_ref, nat, tra, out_t, grad_t, grad_key, grad_value):
    tokens, width = got_ref.shape
    part = width // 4
    size = part // heads
    scale = size ** -0.5
    got = got_ref[...]
    got_t = got.T
    for n in range(4):
        for h in range(heads):
            at = n * part + h * size
            nat[n, h] = got[:, at : at + size]
            piece = got_t[at : at + size]
            tra[n, h] = piece * jnp.asarray(scale, BF16) if n == 0 else piece
    blocks = tokens // block

    def step(t, carry):
        h = t // blocks
        b = t % blocks
        at = pl.multiple_of(b * block, block)
        here = pl.ds(at, block)
        scores = dot(nat[1, h], tra[0, h, :, here])
        lifted = jnp.exp(scores - jnp.max(scores, axis=0, keepdims=True))
        prob = lifted * (1.0 / jnp.sum(lifted, axis=0, keepdims=True))
        prob_half = prob.astype(BF16)
        attended_t = dot(tra[2, h], prob_half).astype(BF16)
        out_t[h, :, here] = attended_t
        grad_out_t = tra[3, h, :, here]
        delta = jnp.sum(grad_out_t.astype(F32) * attended_t.astype(F32), axis=0, keepdims=True)
        grad_prob = dot(nat[2, h], grad_out_t)
        grad_scores = (prob * (grad_prob - delta)).astype(BF16)
        grad_t[h, :, here] = dot(tra[1, h], grad_scores) * scale
        key_terms = dot(grad_scores, nat[0, h, here, :])
        value_terms = dot(prob_half, nat[3, h, here, :])

        @pl.when(b == 0)
        def _():
            grad_key[h] = key_terms
            grad_value[h] = value_terms

        @pl.when(b > 0)
        def _():
            grad_key[h] += key_terms
            grad_value[h] += value_terms

        return carry

    lax.fori_loop(0, heads * blocks, step, 0)
    back_ref[:, :part * 2] = jnp.concatenate(
        [out_t[h].astype(F32) for h in range(heads)] + [grad_t[h] for h in range(heads)], axis=0
    ).T.astype(BF16)
    back_ref[:, part * 2:] = jnp.concatenate(
        [grad_key[h] * scale for h in range(heads)] + [grad_value[h] for h in range(heads)], axis=1
    ).astype(BF16)


def time_backward_kernel(
    both_ref, back_ref, hidden_ref, qkv_ref, attended_ref, prob_ref, gain_time_ref, gain_space_ref,
    qkv_time_hbm, out_time_hbm, qkv_space_hbm, out_space_hbm,
    out_ref,
    qkv_time_ref, out_time_ref, qkv_space_ref, out_space_ref, sems,
):
    copies = [
        pltpu.make_async_copy(src, dst, sems.at[n])
        for n, (src, dst) in enumerate((
            (out_space_hbm, out_space_ref), (qkv_space_hbm, qkv_space_ref),
            (out_time_hbm, out_time_ref), (qkv_time_hbm, qkv_time_ref),
        ))
    ]
    for copy in copies:
        copy.start()
    tokens, features = hidden_ref.shape
    groups = back_ref.shape[0]
    part = features // groups
    size = features // HEADS
    scale = size ** -0.5
    shape = (both_ref.shape[0],) + both_ref.shape[2:]

    def column(n):
        return jnp.concatenate(
            [back_ref[g, :, n * part : (n + 1) * part] for g in range(groups)], axis=1
        )

    hidden = hidden_ref[...].astype(F32)
    copies[0].wait()
    block_output = (hidden + dot(column(0), out_space_ref[...])).astype(BF16)
    out_ref[:, 0] = block_output.reshape(shape)
    grad_qkv = jnp.concatenate([column(1), column(2), column(3)], axis=1)
    copies[1].wait()
    grad_normed = dot_last(grad_qkv, qkv_space_ref[...])
    normed, inverse = norm_stats(hidden)
    cotangent = both_ref[:, 1].reshape(tokens, features).astype(F32)
    grad_hidden = (
        cotangent + norm_backward(grad_normed, gain_space_ref[...], normed, inverse)
    ).astype(BF16)
    copies[2].wait()
    grad_out = dot_last(grad_hidden, out_time_ref[...]).astype(BF16)
    qkv = qkv_ref[...]
    keys_t = qkv[:, features : 2 * features].T
    grad_out_t = grad_out.T
    product_t = (grad_out.astype(F32) * attended_ref[...].astype(F32)).T
    queries_grad, keys_grad, values_grad = [], [], []
    for h in range(HEADS):
        own = slice(h * size, (h + 1) * size)
        delta = jnp.sum(product_t[own], axis=0, keepdims=True)
        prob = prob_ref[h]
        values = qkv[:, 2 * features + h * size : 2 * features + (h + 1) * size]
        grad_prob = dot(values, grad_out_t[own])
        grad_scores = (prob.astype(F32) * (grad_prob - delta)).astype(BF16)
        queries_grad.append(dot(keys_t[own], grad_scores) * scale)
        keys_grad.append(dot(grad_scores, qkv[:, own]) * scale)
        values_grad.append(dot(prob, grad_out[:, own]))
    grad_qkv_time = jnp.concatenate(
        [
            jnp.concatenate(queries_grad, axis=0).T.astype(BF16),
            jnp.concatenate(keys_grad, axis=1).astype(BF16),
            jnp.concatenate(values_grad, axis=1).astype(BF16),
        ],
        axis=1,
    )
    copies[3].wait()
    grad_normed_time = dot_last(grad_qkv_time, qkv_time_ref[...])
    tokens_in = both_ref[:, 0].reshape(tokens, features).astype(F32)
    normed_time, inverse_time = norm_stats(tokens_in)
    input_grad = grad_hidden.astype(F32) + norm_backward(
        grad_normed_time, gain_time_ref[...], normed_time, inverse_time
    )
    out_ref[:, 1] = input_grad.astype(BF16).reshape(shape)


def local(
    frame_count, tile_count,
    patch_tokens, gain_time, qkv_time, out_time, gain_space, qkv_space, out_space, cotangent,
):
    frames, patches, features = patch_tokens.shape
    devices = frame_count * tile_count
    own_patches = patches // frame_count
    all_frames = frames * frame_count
    tokens = all_frames * own_patches
    groups = devices // all_frames
    heads = HEADS // groups
    part = features // groups
    params = pltpu.CompilerParams(vmem_limit_bytes=LIMIT)
    gain_time, gain_space = gain_time[None], gain_space[None]
    weights = (qkv_time, out_time, qkv_space, out_space)

    def shaped(shape, dtype=BF16):
        return jax.ShapeDtypeStruct(shape, dtype)

    both = jnp.stack([patch_tokens, cotangent])
    both = both.reshape(2, frames, frame_count, own_patches, features).transpose(2, 0, 1, 3, 4)
    both = lax.all_to_all(both, "frame", 0, 0)
    both = both.reshape(frame_count, 2, frames * own_patches, features)

    weight_scratch = [pltpu.VMEM(w.shape, w.dtype) for w in weights] + [pltpu.SemaphoreType.DMA((4,))]
    send, hidden, qkv, attended, prob = pl.pallas_call(
        functools.partial(time_forward_kernel, own_patches, groups),
        out_shape=(
            shaped((groups, tokens, 4 * part)),
            shaped((tokens, features)),
            shaped((tokens, 3 * features)),
            shaped((tokens, features)),
            shaped((HEADS, tokens, tokens)),
        ),
        in_specs=[VMEM] * 3 + [ANY] * 4,
        out_specs=[VMEM] * 5,
        scratch_shapes=weight_scratch,
        compiler_params=params,
        name="time_forward",
    )(both, gain_time, gain_space, *weights)

    got = lax.all_to_all(
        send.reshape(devices, own_patches, 4 * part), ("frame", "tile"), 0, 0
    ).reshape(devices * own_patches, 4 * part)

    rows = devices * own_patches
    size = features // HEADS
    back = pl.pallas_call(
        functools.partial(space_kernel, heads, 256),
        out_shape=shaped((rows, 4 * part)),
        in_specs=[VMEM],
        out_specs=VMEM,
        scratch_shapes=[
            pltpu.VMEM((4, heads, rows, size), BF16),
            pltpu.VMEM((4, heads, size, rows), BF16),
            pltpu.VMEM((heads, size, rows), BF16),
            pltpu.VMEM((heads, size, rows), F32),
            pltpu.VMEM((heads, rows, size), F32),
            pltpu.VMEM((heads, rows, size), F32),
        ],
        compiler_params=params,
        name="space_attention",
    )(got)

    back = lax.all_to_all(
        back.reshape(devices, own_patches, 4 * part), ("frame", "tile"), 0, 0
    ).reshape(groups, tokens, 4 * part)

    result = pl.pallas_call(
        time_backward_kernel,
        out_shape=shaped(both.shape),
        in_specs=[VMEM] * 8 + [ANY] * 4,
        out_specs=VMEM,
        scratch_shapes=weight_scratch,
        compiler_params=params,
        name="time_backward",
    )(both, back, hidden, qkv, attended, prob, gain_time, gain_space, *weights)

    result = lax.all_to_all(result, "frame", 0, 0)
    result = result.reshape(frame_count, 2, frames, own_patches, features).transpose(1, 2, 0, 3, 4)
    result = result.reshape(2, frames, patches, features)
    return result[0], result[1]


def solution(mesh):
    in_specs = (P("frame", "tile", None), P(), P(), P(), P(), P(), P(), P("frame", "tile", None))
    out_specs = (P("frame", "tile", None), P("frame", "tile", None))
    return jax.shard_map(
        functools.partial(local, mesh.shape["frame"], mesh.shape["tile"]),
        mesh=mesh, in_specs=in_specs, out_specs=out_specs, check_vma=False,
    )
```

```python
import functools

import jax
import jax.numpy as jnp
from jax import lax
from jax.experimental import pallas as pl
from jax.experimental.pallas import tpu as pltpu
from jax.sharding import PartitionSpec as P

HEADS = 12
EPSILON = 1e-05
F32 = jnp.float32
BF16 = jnp.bfloat16
VMEM = pl.BlockSpec(memory_space=pltpu.VMEM)
HBM = pl.BlockSpec(memory_space=pltpu.HBM)
LIMIT = 32 * 1024 * 1024


def dot(a, b):
    return jnp.dot(a, b, preferred_element_type=F32)


def dot_last(a, b):
    return lax.dot_general(a, b, (((1,), (1,)), ((), ())), preferred_element_type=F32)


def norm_stats(wide):
    average = jnp.mean(wide, axis=-1, keepdims=True)
    centred = wide - average
    inverse = lax.rsqrt(jnp.mean(centred * centred, axis=-1, keepdims=True) + EPSILON)
    return centred * inverse, inverse


def norm_backward(grad_normed, gain, normed, inverse):
    scaled = grad_normed * gain
    return inverse * (
        scaled
        - jnp.mean(scaled, axis=-1, keepdims=True)
        - normed * jnp.mean(scaled * normed, axis=-1, keepdims=True)
    )


def same_patch(tokens, patches):
    rows = lax.broadcasted_iota(jnp.int32, (tokens, tokens), 0)
    columns = lax.broadcasted_iota(jnp.int32, (tokens, tokens), 1)
    return (rows % patches) == (columns % patches)


def time_forward_kernel(
    patches, groups,
    both_ref, gain_time_ref, gain_space_ref, qkv_time_hbm, out_time_ref, qkv_space_hbm, out_space_ref,
    send_ref, hidden_ref, qkv_ref, attended_ref, prob_ref,
    qkv_time_ref, qkv_space_ref, sems,
):
    copies = [
        pltpu.make_async_copy(src, dst, sems.at[n])
        for n, (src, dst) in enumerate(
            ((qkv_time_hbm, qkv_time_ref), (qkv_space_hbm, qkv_space_ref))
        )
    ]
    for copy in copies:
        copy.start()
    tokens, features = hidden_ref.shape
    size = features // HEADS
    part = features // groups
    tokens_in = both_ref[:, 0].reshape(tokens, features).astype(F32)
    cotangent = both_ref[:, 1].reshape(tokens, features)
    normed, _ = norm_stats(tokens_in)
    normed_half = (normed * gain_time_ref[...]).astype(BF16)
    copies[0].wait()
    qkv = dot(normed_half, qkv_time_ref[...]).astype(BF16)
    qkv_ref[...] = qkv
    grad_out = dot_last(cotangent, out_space_ref[...]).astype(BF16)
    qkv_t = qkv.T
    mask = same_patch(tokens, patches)
    outputs = []
    for h in range(HEADS):
        keys = qkv[:, features + h * size : features + (h + 1) * size]
        queries_t = qkv_t[h * size : (h + 1) * size] * jnp.asarray(size ** -0.5, BF16)
        scores = jnp.where(mask, dot(keys, queries_t), -1e30)
        lifted = jnp.exp(scores - jnp.max(scores, axis=0, keepdims=True))
        prob = (lifted / jnp.sum(lifted, axis=0, keepdims=True)).astype(BF16)
        prob_ref[h] = prob
        values_t = qkv_t[2 * features + h * size : 2 * features + (h + 1) * size]
        outputs.append(dot(values_t, prob))
    attended = jnp.concatenate(outputs, axis=0).T.astype(BF16)
    attended_ref[...] = attended
    hidden = (tokens_in + dot(attended, out_time_ref[...])).astype(BF16)
    hidden_ref[...] = hidden
    normed_space, _ = norm_stats(hidden.astype(F32))
    space_half = (normed_space * gain_space_ref[...]).astype(BF16)
    copies[1].wait()
    space = dot(space_half, qkv_space_ref[...]).astype(BF16)
    for g in range(groups):
        send_ref[g] = jnp.concatenate(
            [space[:, n * features + g * part : n * features + (g + 1) * part] for n in range(3)]
            + [grad_out[:, g * part : (g + 1) * part]],
            axis=1,
        )


def space_kernel(
    heads, block, together, got_ref, back_ref, nat, tra, out_t, grad_t, grad_key, grad_value
):
    tokens, width = got_ref.shape
    part = width // 4
    size = part // heads
    scale = size ** -0.5
    got = got_ref[...]
    got_t = got.T
    for n in range(4):
        for h in range(heads):
            at = n * part + h * size
            if n in (1, 2):
                nat[n - 1, h] = got[:, at : at + size]
            piece = got_t[at : at + size]
            tra[n, h, :size] = piece * jnp.asarray(scale, BF16) if n == 0 else piece
            if n == 2:
                tra[n, h, size:] = jnp.ones((tra.shape[2] - size, tokens), BF16)
    grad_key[...] = jnp.zeros_like(grad_key)
    grad_value[...] = jnp.zeros_like(grad_value)
    blocks = tokens // block

    def attention(t):
        h = t // blocks
        here = pl.ds(pl.multiple_of(t % blocks * block, block), block)
        query_t = tra[0, h, :size, here]
        grad_out_t = tra[3, h, :size, here]
        scores = dot(nat[0, h], query_t)
        yield
        weights = jnp.exp(scores - jnp.max(scores, axis=0, keepdims=True)).astype(BF16)
        yield
        sums = dot(tra[2, h], weights)
        inverse = 1.0 / sums[size : size + 1]
        attended_t = (sums[:size] * inverse).astype(BF16)
        out_t[h, :, here] = attended_t
        delta = jnp.sum(grad_out_t.astype(F32) * attended_t.astype(F32), axis=0, keepdims=True)
        grad_prob = dot(nat[1, h], grad_out_t)
        grad_scores = (weights.astype(F32) * (grad_prob - delta)).astype(BF16)
        yield
        grad_t[h, :, here] = dot(tra[1, h, :size], grad_scores) * (inverse * scale)
        grad_key[h] += dot_last(grad_scores, (query_t.astype(F32) * inverse).astype(BF16))
        grad_value[h] += dot_last(weights, (grad_out_t.astype(F32) * inverse).astype(BF16))
        yield

    def step(t, carry):
        running = [attention(t * together + n) for n in range(together)]
        for _ in range(4):
            for one in running:
                next(one)
        return carry

    lax.fori_loop(0, heads * blocks // together, step, 0)
    back_ref[:, : part * 2] = jnp.concatenate(
        [out_t[h].astype(F32) for h in range(heads)] + [grad_t[h] for h in range(heads)], axis=0
    ).T.astype(BF16)
    back_ref[:, part * 2 :] = jnp.concatenate(
        [grad_key[h] for h in range(heads)] + [grad_value[h] for h in range(heads)], axis=1
    ).astype(BF16)


def time_backward_kernel(
    both_ref, back_ref, hidden_ref, qkv_ref, attended_ref, prob_ref, gain_time_ref, gain_space_ref,
    qkv_time_ref, out_time_ref, qkv_space_ref, out_space_ref, out_ref,
):
    tokens, features = hidden_ref.shape
    groups = back_ref.shape[0]
    part = features // groups
    size = features // HEADS
    scale = size ** -0.5
    shape = (both_ref.shape[0],) + both_ref.shape[2:]

    def column(n):
        return jnp.concatenate(
            [back_ref[g, :, n * part : (n + 1) * part] for g in range(groups)], axis=1
        )

    hidden = hidden_ref[...].astype(F32)
    block_output = (hidden + dot(column(0), out_space_ref[...])).astype(BF16)
    out_ref[:, 0] = block_output.reshape(shape)
    grad_qkv = jnp.concatenate([column(1), column(2), column(3)], axis=1)
    grad_normed = dot_last(grad_qkv, qkv_space_ref[...])
    normed, inverse = norm_stats(hidden)
    cotangent = both_ref[:, 1].reshape(tokens, features).astype(F32)
    grad_hidden = (
        cotangent + norm_backward(grad_normed, gain_space_ref[...], normed, inverse)
    ).astype(BF16)
    grad_out = dot_last(grad_hidden, out_time_ref[...]).astype(BF16)
    qkv = qkv_ref[...]
    keys_t = qkv[:, features : 2 * features].T
    grad_out_t = grad_out.T
    product_t = (grad_out.astype(F32) * attended_ref[...].astype(F32)).T
    queries_grad, keys_grad, values_grad = [], [], []
    for h in range(HEADS):
        own = slice(h * size, (h + 1) * size)
        delta = jnp.sum(product_t[own], axis=0, keepdims=True)
        prob = prob_ref[h]
        values = qkv[:, 2 * features + h * size : 2 * features + (h + 1) * size]
        grad_prob = dot(values, grad_out_t[own])
        grad_scores = (prob.astype(F32) * (grad_prob - delta)).astype(BF16)
        queries_grad.append(dot(keys_t[own], grad_scores) * scale)
        keys_grad.append(dot(grad_scores, qkv[:, own]) * scale)
        values_grad.append(dot(prob, grad_out[:, own]))
    grad_qkv_time = jnp.concatenate(
        [
            jnp.concatenate(queries_grad, axis=0).T.astype(BF16),
            jnp.concatenate(keys_grad, axis=1).astype(BF16),
            jnp.concatenate(values_grad, axis=1).astype(BF16),
        ],
        axis=1,
    )
    grad_normed_time = dot_last(grad_qkv_time, qkv_time_ref[...])
    tokens_in = both_ref[:, 0].reshape(tokens, features).astype(F32)
    normed_time, inverse_time = norm_stats(tokens_in)
    input_grad = grad_hidden.astype(F32) + norm_backward(
        grad_normed_time, gain_time_ref[...], normed_time, inverse_time
    )
    out_ref[:, 1] = input_grad.astype(BF16).reshape(shape)


def local(
    frame_count, tile_count,
    patch_tokens, gain_time, qkv_time, out_time, gain_space, qkv_space, out_space, cotangent,
):
    frames, patches, features = patch_tokens.shape
    devices = frame_count * tile_count
    own_patches = patches // frame_count
    all_frames = frames * frame_count
    tokens = all_frames * own_patches
    groups = devices // all_frames
    heads = HEADS // groups
    part = features // groups
    params = pltpu.CompilerParams(vmem_limit_bytes=LIMIT)
    weights = (qkv_time, out_time, qkv_space, out_space)
    far = lambda w: pltpu.with_memory_space_constraint(w, pltpu.HBM)

    def shaped(shape, dtype=BF16):
        return jax.ShapeDtypeStruct(shape, dtype)

    both = jnp.stack([patch_tokens, cotangent])
    both = both.reshape(2, frames, frame_count, own_patches, features).transpose(2, 0, 1, 3, 4)
    both = lax.all_to_all(both, "frame", 0, 0)
    both = both.reshape(frame_count, 2, frames * own_patches, features)

    send, hidden, qkv, attended, prob = pl.pallas_call(
        functools.partial(time_forward_kernel, own_patches, groups),
        out_shape=(
            shaped((groups, tokens, 4 * part)),
            shaped((tokens, features)),
            shaped((tokens, 3 * features)),
            shaped((tokens, features)),
            shaped((HEADS, tokens, tokens)),
        ),
        in_specs=[VMEM] * 3 + [HBM, VMEM, HBM, VMEM],
        out_specs=[VMEM] * 5,
        scratch_shapes=[
            pltpu.VMEM(qkv_time.shape, BF16),
            pltpu.VMEM(qkv_space.shape, BF16),
            pltpu.SemaphoreType.DMA((2,)),
        ],
        compiler_params=params,
        name="time_forward",
    )(both, gain_time, gain_space, far(qkv_time), out_time, far(qkv_space), out_space)

    got = lax.all_to_all(
        send.reshape(devices, own_patches, 4 * part), ("frame", "tile"), 0, 0
    ).reshape(devices * own_patches, 4 * part)

    rows = devices * own_patches
    size = features // HEADS
    back = pl.pallas_call(
        functools.partial(space_kernel, heads, 256, 4),
        out_shape=shaped((rows, 4 * part)),
        in_specs=[VMEM],
        out_specs=VMEM,
        scratch_shapes=[
            pltpu.VMEM((2, heads, rows, size), BF16),
            pltpu.VMEM((4, heads, size + 16, rows), BF16),
            pltpu.VMEM((heads, size, rows), BF16),
            pltpu.VMEM((heads, size, rows), F32),
            pltpu.VMEM((heads, rows, size), F32),
            pltpu.VMEM((heads, rows, size), F32),
        ],
        compiler_params=params,
        name="space_attention",
    )(got)

    back = lax.all_to_all(
        back.reshape(devices, own_patches, 4 * part), ("frame", "tile"), 0, 0
    ).reshape(groups, tokens, 4 * part)

    result = pl.pallas_call(
        time_backward_kernel,
        out_shape=shaped(both.shape),
        in_specs=[VMEM] * 12,
        out_specs=VMEM,
        compiler_params=params,
        name="time_backward",
    )(both, back, hidden, qkv, attended, prob, gain_time, gain_space, *weights)

    result = lax.all_to_all(result, "frame", 0, 0)
    result = result.reshape(frame_count, 2, frames, own_patches, features).transpose(1, 2, 0, 3, 4)
    result = result.reshape(2, frames, patches, features)
    return result[0], result[1]


def solution(mesh):
    in_specs = (P("frame", "tile", None), P(), P(), P(), P(), P(), P(), P("frame", "tile", None))
    out_specs = (P("frame", "tile", None), P("frame", "tile", None))
    return jax.shard_map(
        functools.partial(local, mesh.shape["frame"], mesh.shape["tile"]),
        mesh=mesh, in_specs=in_specs, out_specs=out_specs, check_vma=False,
    )
```

```python
import functools

import jax
import jax.numpy as jnp
from jax import lax
from jax.experimental import pallas as pl
from jax.experimental.pallas import tpu as pltpu
from jax.sharding import PartitionSpec as P

HEADS = 12
EPSILON = 1e-05
F32 = jnp.float32
BF16 = jnp.bfloat16
VMEM = pl.BlockSpec(memory_space=pltpu.VMEM)
HBM = pl.BlockSpec(memory_space=pltpu.HBM)
LIMIT = 32 * 1024 * 1024


def dot(a, b):
    return jnp.dot(a, b, preferred_element_type=F32)


def dot_last(a, b):
    return lax.dot_general(a, b, (((1,), (1,)), ((), ())), preferred_element_type=F32)


def norm_stats(wide):
    average = jnp.mean(wide, axis=-1, keepdims=True)
    centred = wide - average
    inverse = lax.rsqrt(jnp.mean(centred * centred, axis=-1, keepdims=True) + EPSILON)
    return centred * inverse, inverse


def norm_backward(grad_normed, gain, normed, inverse):
    scaled = grad_normed * gain
    return inverse * (
        scaled
        - jnp.mean(scaled, axis=-1, keepdims=True)
        - normed * jnp.mean(scaled * normed, axis=-1, keepdims=True)
    )


def in_turn(running):
    running, ended = list(running), {}
    while len(ended) < len(running):
        for n, one in enumerate(running):
            if n not in ended:
                try:
                    next(one)
                except StopIteration as stop:
                    ended[n] = stop.value
    return [ended[n] for n in range(len(running))]


def fetch_kernel(qkv_hbm, query_ref, key_ref, sems):
    depth = qkv_hbm.shape[0]
    copies = [
        pltpu.make_async_copy(qkv_hbm.at[:, pl.ds(n * depth, depth)], ref, sems.at[n])
        for n, ref in enumerate((query_ref, key_ref))
    ]
    for copy in copies:
        copy.start()
    for copy in copies:
        copy.wait()


def time_forward_kernel(
    patches, groups, together,
    both_ref, gain_time_ref, gain_space_ref, query_time_ref, key_time_ref,
    qkv_time_hbm, out_time_hbm, qkv_space_hbm, out_space_hbm,
    send_ref, hidden_ref, qkv_ref, attended_ref, weights_ref, inverse_ref,
    value_time_ref, out_space_ref, out_time_ref, qkv_space_ref, sems,
):
    depth = qkv_time_hbm.shape[0]
    copies = [
        pltpu.make_async_copy(src, dst, sems.at[n])
        for n, (src, dst) in enumerate((
            (qkv_time_hbm.at[:, pl.ds(2 * depth, depth)], value_time_ref),
            (out_space_hbm, out_space_ref),
            (out_time_hbm, out_time_ref),
            (qkv_space_hbm, qkv_space_ref),
        ))
    ]
    for copy in copies:
        copy.start()
    tokens, features = hidden_ref.shape
    size = features // HEADS
    part = features // groups
    tokens_in = both_ref[:, 0].reshape(tokens, features).astype(F32)
    cotangent = both_ref[:, 1].reshape(tokens, features)
    normed, _ = norm_stats(tokens_in)
    normed_half = (normed * gain_time_ref[...]).astype(BF16)
    queries = dot(normed_half, query_time_ref[...]).astype(BF16)
    keys = dot(normed_half, key_time_ref[...]).astype(BF16)
    copies[0].wait()
    values = dot(normed_half, value_time_ref[...]).astype(BF16)
    qkv = jnp.concatenate([queries, keys, values], axis=1)
    qkv_ref[...] = qkv
    copies[1].wait()
    grad_out = dot_last(cotangent, out_space_ref[...]).astype(BF16)
    qkv_t = qkv.T
    queries_t = qkv_t[:features] * jnp.asarray(size ** -0.5, BF16)
    rows = lax.broadcasted_iota(jnp.int32, (tokens, tokens), 0)
    columns = lax.broadcasted_iota(jnp.int32, (tokens, tokens), 1)
    bias = jnp.where((rows % patches) == (columns % patches), 0.0, -1e30)
    ones = jnp.ones((16, tokens), BF16)

    def attention(h):
        keys = qkv[:, features + h * size : features + (h + 1) * size]
        scores = dot(keys, queries_t[h * size : (h + 1) * size]) + bias
        yield
        weights = jnp.exp(scores - jnp.max(scores, axis=0, keepdims=True)).astype(BF16)
        weights_ref[h] = weights
        yield
        values_t = qkv_t[2 * features + h * size : 2 * features + (h + 1) * size]
        sums = dot(jnp.concatenate([values_t, ones], axis=0), weights)
        inverse = 1.0 / sums[size : size + 1]
        inverse_ref[h : h + 1] = inverse
        return sums[:size] * inverse

    outputs = []
    for h in range(0, HEADS, together):
        outputs += in_turn(attention(h + n) for n in range(together))
    attended = jnp.concatenate(outputs, axis=0).T.astype(BF16)
    attended_ref[...] = attended
    copies[2].wait()
    hidden = (tokens_in + dot(attended, out_time_ref[...])).astype(BF16)
    hidden_ref[...] = hidden
    normed_space, _ = norm_stats(hidden.astype(F32))
    space_half = (normed_space * gain_space_ref[...]).astype(BF16)
    copies[3].wait()
    space = dot(space_half, qkv_space_ref[...]).astype(BF16)
    for g in range(groups):
        send_ref[g] = jnp.concatenate(
            [space[:, n * features + g * part : n * features + (g + 1) * part] for n in range(3)]
            + [grad_out[:, g * part : (g + 1) * part]],
            axis=1,
        )


def space_kernel(
    heads, block, together, got_ref, back_ref, nat, tra, out_t, grad_t, grad_key, grad_value
):
    tokens, width = got_ref.shape
    part = width // 4
    size = part // heads
    scale = size ** -0.5
    got = got_ref[...]
    got_t = got.T
    for n in range(4):
        for h in range(heads):
            at = n * part + h * size
            if n in (1, 2):
                nat[n - 1, h] = got[:, at : at + size]
            piece = got_t[at : at + size]
            tra[n, h, :size] = piece * jnp.asarray(scale, BF16) if n == 0 else piece
            if n == 2:
                tra[n, h, size:] = jnp.ones((tra.shape[2] - size, tokens), BF16)
    grad_key[...] = jnp.zeros_like(grad_key)
    grad_value[...] = jnp.zeros_like(grad_value)
    blocks = tokens // block

    def attention(t):
        h = t // blocks
        here = pl.ds(pl.multiple_of(t % blocks * block, block), block)
        query_t = tra[0, h, :size, here]
        grad_out_t = tra[3, h, :size, here]
        scores = dot(nat[0, h], query_t)
        yield
        weights = jnp.exp(scores - jnp.max(scores, axis=0, keepdims=True)).astype(BF16)
        yield
        sums = dot(tra[2, h], weights)
        inverse = 1.0 / sums[size : size + 1]
        attended_t = (sums[:size] * inverse).astype(BF16)
        out_t[h, :, here] = attended_t
        delta = jnp.sum(grad_out_t.astype(F32) * attended_t.astype(F32), axis=0, keepdims=True)
        grad_prob = dot(nat[1, h], grad_out_t)
        grad_scores = (weights.astype(F32) * (grad_prob - delta)).astype(BF16)
        yield
        grad_t[h, :, here] = dot(tra[1, h, :size], grad_scores) * (inverse * scale)
        grad_key[h] += dot_last(grad_scores, (query_t.astype(F32) * inverse).astype(BF16))
        grad_value[h] += dot_last(weights, (grad_out_t.astype(F32) * inverse).astype(BF16))

    def step(t, carry):
        in_turn(attention(t * together + n) for n in range(together))
        return carry

    lax.fori_loop(0, heads * blocks // together, step, 0)
    back_ref[:, : part * 2] = jnp.concatenate(
        [out_t[h].astype(F32) for h in range(heads)] + [grad_t[h] for h in range(heads)], axis=0
    ).T.astype(BF16)
    back_ref[:, part * 2 :] = jnp.concatenate(
        [grad_key[h] for h in range(heads)] + [grad_value[h] for h in range(heads)], axis=1
    ).astype(BF16)


def time_backward_kernel(
    together,
    both_ref, back_ref, hidden_ref, qkv_ref, attended_ref, weights_ref, inverse_ref, gain_time_ref, gain_space_ref,
    qkv_time_ref, out_time_ref, qkv_space_ref, out_space_ref, out_ref,
):
    tokens, features = hidden_ref.shape
    groups = back_ref.shape[0]
    part = features // groups
    size = features // HEADS
    scale = size ** -0.5
    shape = (both_ref.shape[0],) + both_ref.shape[2:]

    def column(n):
        return jnp.concatenate(
            [back_ref[g, :, n * part : (n + 1) * part] for g in range(groups)], axis=1
        )

    hidden = hidden_ref[...].astype(F32)
    block_output = (hidden + dot(column(0), out_space_ref[...])).astype(BF16)
    out_ref[:, 0] = block_output.reshape(shape)
    grad_qkv = jnp.concatenate([column(1), column(2), column(3)], axis=1)
    grad_normed = dot_last(grad_qkv, qkv_space_ref[...])
    normed, inverse = norm_stats(hidden)
    cotangent = both_ref[:, 1].reshape(tokens, features).astype(F32)
    grad_hidden = (
        cotangent + norm_backward(grad_normed, gain_space_ref[...], normed, inverse)
    ).astype(BF16)
    grad_out = dot_last(grad_hidden, out_time_ref[...]).astype(BF16)
    qkv = qkv_ref[...]
    keys_t = qkv[:, features : 2 * features].T
    grad_out_t = grad_out.T
    product_t = (grad_out.astype(F32) * attended_ref[...].astype(F32)).T
    queries_t = qkv[:, :features].T

    def attention(h):
        own = slice(h * size, (h + 1) * size)
        delta = jnp.sum(product_t[own], axis=0, keepdims=True)
        weights = weights_ref[h]
        inverse = inverse_ref[h : h + 1]
        values = qkv[:, 2 * features + h * size : 2 * features + (h + 1) * size]
        grad_prob = dot(values, grad_out_t[own])
        yield
        grad_scores = (weights.astype(F32) * (grad_prob - delta)).astype(BF16)
        yield
        queries_grad = dot(keys_t[own], grad_scores) * (inverse * scale)
        keys_grad = dot_last(grad_scores, (queries_t[own].astype(F32) * inverse).astype(BF16))
        values_grad = dot_last(weights, (grad_out_t[own].astype(F32) * inverse).astype(BF16))
        return queries_grad, keys_grad * scale, values_grad

    ended = []
    for h in range(0, HEADS, together):
        ended += in_turn(attention(h + n) for n in range(together))
    queries_grad, keys_grad, values_grad = zip(*ended)
    grad_qkv_time = jnp.concatenate(
        [
            jnp.concatenate(queries_grad, axis=0).T.astype(BF16),
            jnp.concatenate(keys_grad, axis=1).astype(BF16),
            jnp.concatenate(values_grad, axis=1).astype(BF16),
        ],
        axis=1,
    )
    grad_normed_time = dot_last(grad_qkv_time, qkv_time_ref[...])
    tokens_in = both_ref[:, 0].reshape(tokens, features).astype(F32)
    normed_time, inverse_time = norm_stats(tokens_in)
    input_grad = grad_hidden.astype(F32) + norm_backward(
        grad_normed_time, gain_time_ref[...], normed_time, inverse_time
    )
    out_ref[:, 1] = input_grad.astype(BF16).reshape(shape)


def local(
    frame_count, tile_count,
    patch_tokens, gain_time, qkv_time, out_time, gain_space, qkv_space, out_space, cotangent,
):
    frames, patches, features = patch_tokens.shape
    devices = frame_count * tile_count
    own_patches = patches // frame_count
    all_frames = frames * frame_count
    tokens = all_frames * own_patches
    groups = devices // all_frames
    heads = HEADS // groups
    part = features // groups
    params = pltpu.CompilerParams(vmem_limit_bytes=LIMIT)
    def shaped(shape, dtype=BF16):
        return jax.ShapeDtypeStruct(shape, dtype)

    weights = (qkv_time, out_time, qkv_space, out_space)
    far = [pltpu.with_memory_space_constraint(w, pltpu.HBM) for w in weights]
    near = pl.pallas_call(
        fetch_kernel,
        out_shape=(shaped((features, features)),) * 2,
        in_specs=[HBM],
        out_specs=[VMEM] * 2,
        scratch_shapes=[pltpu.SemaphoreType.DMA((2,))],
        compiler_params=pltpu.CompilerParams(vmem_limit_bytes=8 * 1024 * 1024),
        cost_estimate=pl.CostEstimate(flops=0, bytes_accessed=20 * 1024 * 1024, transcendentals=0),
        name="fetch_weights",
    )(far[0])

    both = jnp.stack([patch_tokens, cotangent])
    both = both.reshape(2, frames, frame_count, own_patches, features).transpose(2, 0, 1, 3, 4)
    both = lax.all_to_all(both, "frame", 0, 0)
    both = both.reshape(frame_count, 2, frames * own_patches, features)

    send, hidden, qkv, attended, scores, inverse = pl.pallas_call(
        functools.partial(time_forward_kernel, own_patches, groups, 6),
        out_shape=(
            shaped((groups, tokens, 4 * part)),
            shaped((tokens, features)),
            shaped((tokens, 3 * features)),
            shaped((tokens, features)),
            shaped((HEADS, tokens, tokens)),
            shaped((HEADS, tokens), F32),
        ),
        in_specs=[VMEM] * 5 + [HBM] * 4,
        out_specs=[VMEM] * 6,
        scratch_shapes=[
            pltpu.VMEM((features, features), BF16),
            pltpu.VMEM((features, features), BF16),
            pltpu.VMEM((features, features), BF16),
            pltpu.VMEM(qkv_space.shape, BF16),
            pltpu.SemaphoreType.DMA((4,)),
        ],
        compiler_params=params,
        name="time_forward",
    )(both, gain_time, gain_space, *near, *far)

    got = lax.all_to_all(
        send.reshape(devices, own_patches, 4 * part), ("frame", "tile"), 0, 0
    ).reshape(devices * own_patches, 4 * part)

    rows = devices * own_patches
    size = features // HEADS
    back = pl.pallas_call(
        functools.partial(space_kernel, heads, 256, 12),
        out_shape=shaped((rows, 4 * part)),
        in_specs=[VMEM],
        out_specs=VMEM,
        scratch_shapes=[
            pltpu.VMEM((2, heads, rows, size), BF16),
            pltpu.VMEM((4, heads, size + 16, rows), BF16),
            pltpu.VMEM((heads, size, rows), BF16),
            pltpu.VMEM((heads, size, rows), F32),
            pltpu.VMEM((heads, rows, size), F32),
            pltpu.VMEM((heads, rows, size), F32),
        ],
        compiler_params=params,
        name="space_attention",
    )(got)

    back = lax.all_to_all(
        back.reshape(devices, own_patches, 4 * part), ("frame", "tile"), 0, 0
    ).reshape(groups, tokens, 4 * part)

    result = pl.pallas_call(
        functools.partial(time_backward_kernel, 6),
        out_shape=shaped(both.shape),
        in_specs=[VMEM] * 13,
        out_specs=VMEM,
        compiler_params=params,
        name="time_backward",
    )(both, back, hidden, qkv, attended, scores, inverse, gain_time, gain_space, *weights)

    result = lax.all_to_all(result, "frame", 0, 0)
    result = result.reshape(frame_count, 2, frames, own_patches, features).transpose(1, 2, 0, 3, 4)
    result = result.reshape(2, frames, patches, features)
    return result[0], result[1]


def solution(mesh):
    in_specs = (P("frame", "tile", None), P(), P(), P(), P(), P(), P(), P("frame", "tile", None))
    out_specs = (P("frame", "tile", None), P("frame", "tile", None))
    return jax.shard_map(
        functools.partial(local, mesh.shape["frame"], mesh.shape["tile"]),
        mesh=mesh, in_specs=in_specs, out_specs=out_specs, check_vma=False,
    )
```

```python
import functools

import jax
import jax.numpy as jnp
from jax import lax
from jax.experimental import pallas as pl
from jax.experimental.pallas import tpu as pltpu
from jax.sharding import PartitionSpec as P

HEADS = 12
EPSILON = 1e-05
F32 = jnp.float32
BF16 = jnp.bfloat16
VMEM = pl.BlockSpec(memory_space=pltpu.VMEM)
HBM = pl.BlockSpec(memory_space=pltpu.HBM)
LIMIT = 32 * 1024 * 1024


def dot(a, b):
    return jnp.dot(a, b, preferred_element_type=F32)


def dot_last(a, b):
    return lax.dot_general(a, b, (((1,), (1,)), ((), ())), preferred_element_type=F32)


def norm_stats(wide):
    average = jnp.mean(wide, axis=-1, keepdims=True)
    centred = wide - average
    inverse = lax.rsqrt(jnp.mean(centred * centred, axis=-1, keepdims=True) + EPSILON)
    return centred * inverse, inverse


def norm_backward(grad_normed, gain, normed, inverse):
    scaled = grad_normed * gain
    return inverse * (
        scaled
        - jnp.mean(scaled, axis=-1, keepdims=True)
        - normed * jnp.mean(scaled * normed, axis=-1, keepdims=True)
    )


def in_turn(running):
    running, ended = list(running), {}
    while len(ended) < len(running):
        for n, one in enumerate(running):
            if n not in ended:
                try:
                    next(one)
                except StopIteration as stop:
                    ended[n] = stop.value
    return [ended[n] for n in range(len(running))]


def fetch_kernel(qkv_hbm, query_ref, key_ref, sems):
    depth = qkv_hbm.shape[0]
    copies = [
        pltpu.make_async_copy(qkv_hbm.at[:, pl.ds(n * depth, depth)], ref, sems.at[n])
        for n, ref in enumerate((query_ref, key_ref))
    ]
    for copy in copies:
        copy.start()
    for copy in copies:
        copy.wait()


def time_forward_kernel(
    patches, groups, together,
    both_ref, gain_time_ref, gain_space_ref, query_time_ref, key_time_ref,
    qkv_time_hbm, out_time_hbm, qkv_space_hbm, out_space_hbm,
    send_ref, hidden_ref, qkv_ref, attended_ref, weights_ref, inverse_ref,
    value_time_ref, out_space_ref, out_time_ref, qkv_space_ref, sems,
):
    depth = qkv_time_hbm.shape[0]
    copies = [
        pltpu.make_async_copy(src, dst, sems.at[n])
        for n, (src, dst) in enumerate((
            (qkv_time_hbm.at[:, pl.ds(2 * depth, depth)], value_time_ref),
            (out_space_hbm, out_space_ref),
            (out_time_hbm, out_time_ref),
            (qkv_space_hbm, qkv_space_ref),
        ))
    ]
    for copy in copies:
        copy.start()
    tokens, features = hidden_ref.shape
    size = features // HEADS
    part = features // groups
    tokens_in = both_ref[:, 0].reshape(tokens, features).astype(F32)
    cotangent = both_ref[:, 1].reshape(tokens, features)
    normed, _ = norm_stats(tokens_in)
    normed_half = (normed * gain_time_ref[...]).astype(BF16)
    queries = dot(normed_half, query_time_ref[...]).astype(BF16)
    keys = dot(normed_half, key_time_ref[...]).astype(BF16)
    qkv_ref[:, :features] = queries
    qkv_ref[:, features : 2 * features] = keys
    queries_t = queries.T * jnp.asarray(size ** -0.5, BF16)
    rows = lax.broadcasted_iota(jnp.int32, (tokens, tokens), 0)
    columns = lax.broadcasted_iota(jnp.int32, (tokens, tokens), 1)
    bias = jnp.where((rows % patches) == (columns % patches), 0.0, -1e30)
    ones = jnp.ones((16, tokens), BF16)

    def attention(h):
        own = slice(h * size, (h + 1) * size)
        scores = dot(keys[:, own], queries_t[own]) + bias
        yield
        weights = jnp.exp(scores - jnp.max(scores, axis=0, keepdims=True)).astype(BF16)
        weights_ref[h] = weights
        yield
        sums = dot(jnp.concatenate([values_t[own], ones], axis=0), weights)
        inverse = 1.0 / sums[size : size + 1]
        inverse_ref[h : h + 1] = inverse
        return (sums[:size] * inverse).astype(BF16)

    first = [attention(h) for h in range(together)]
    for one in first:
        next(one)
    copies[0].wait()
    copies[1].wait()
    values = dot(normed_half, value_time_ref[...]).astype(BF16)
    qkv_ref[:, 2 * features :] = values
    values_t = values.T
    grad_out = dot_last(cotangent, out_space_ref[...]).astype(BF16)
    outputs = in_turn(first)
    for h in range(together, HEADS, together):
        outputs += in_turn(attention(h + n) for n in range(together))
    attended = jnp.concatenate(outputs, axis=0).T
    attended_ref[...] = attended
    copies[2].wait()
    hidden = (tokens_in + dot(attended, out_time_ref[...])).astype(BF16)
    hidden_ref[...] = hidden
    normed_space, _ = norm_stats(hidden.astype(F32))
    space_half = (normed_space * gain_space_ref[...]).astype(BF16)
    copies[3].wait()
    space = dot(space_half, qkv_space_ref[...]).astype(BF16)
    for g in range(groups):
        send_ref[g] = jnp.concatenate(
            [space[:, n * features + g * part : n * features + (g + 1) * part] for n in range(3)]
            + [grad_out[:, g * part : (g + 1) * part]],
            axis=1,
        )


def space_kernel(
    heads, block, together, got_ref, back_ref, nat, tra, out_t, grad_t, grad_key, grad_value
):
    tokens, width = got_ref.shape
    part = width // 4
    size = part // heads
    scale = size ** -0.5
    got = got_ref[...]
    got_t = got.T
    for n in range(4):
        for h in range(heads):
            at = n * part + h * size
            if n in (1, 2):
                nat[n - 1, h] = got[:, at : at + size]
            piece = got_t[at : at + size]
            tra[n, h, :size] = piece * jnp.asarray(scale, BF16) if n == 0 else piece
            if n == 2:
                tra[n, h, size:] = jnp.ones((tra.shape[2] - size, tokens), BF16)
    blocks = tokens // block

    def attention(t):
        h = t // blocks
        here = pl.ds(t % blocks * block, block)
        query_t = tra[0, h, :size, here]
        grad_out_t = tra[3, h, :size, here]
        scores = dot(nat[0, h], query_t)
        yield
        weights = jnp.exp(scores - jnp.max(scores, axis=0, keepdims=True)).astype(BF16)
        yield
        sums = dot(tra[2, h], weights)
        inverse = 1.0 / sums[size : size + 1]
        attended_t = (sums[:size] * inverse).astype(BF16)
        out_t[h, :, here] = attended_t
        delta = jnp.sum(grad_out_t.astype(F32) * attended_t.astype(F32), axis=0, keepdims=True)
        grad_prob = dot(nat[1, h], grad_out_t)
        grad_scores = (weights.astype(F32) * (grad_prob - delta)).astype(BF16)
        yield
        grad_t[h, :, here] = (dot(tra[1, h, :size], grad_scores) * (inverse * scale)).astype(BF16)
        key_terms = dot_last(grad_scores, (query_t.astype(F32) * inverse).astype(BF16))
        value_terms = dot_last(weights, (grad_out_t.astype(F32) * inverse).astype(BF16))
        if t % blocks == 0:
            grad_key[h], grad_value[h] = key_terms, value_terms
        else:
            grad_key[h] += key_terms
            grad_value[h] += value_terms

    for t in range(0, heads * blocks, together):
        in_turn(attention(t + n) for n in range(together))
    back_ref[:, : part * 2] = jnp.concatenate(
        [out_t[h] for h in range(heads)] + [grad_t[h] for h in range(heads)], axis=0
    ).T
    back_ref[:, part * 2 :] = jnp.concatenate(
        [grad_key[h] for h in range(heads)] + [grad_value[h] for h in range(heads)], axis=1
    ).astype(BF16)


def time_backward_kernel(
    together,
    both_ref, back_ref, hidden_ref, qkv_ref, attended_ref, weights_ref, inverse_ref, gain_time_ref, gain_space_ref,
    qkv_time_ref, out_time_ref, qkv_space_ref, out_space_ref, out_ref,
):
    tokens, features = hidden_ref.shape
    groups = back_ref.shape[0]
    part = features // groups
    size = features // HEADS
    scale = size ** -0.5
    shape = (both_ref.shape[0],) + both_ref.shape[2:]

    def column(n):
        return jnp.concatenate(
            [back_ref[g, :, n * part : (n + 1) * part] for g in range(groups)], axis=1
        )

    hidden = hidden_ref[...].astype(F32)
    block_output = (hidden + dot(column(0), out_space_ref[...])).astype(BF16)
    out_ref[:, 0] = block_output.reshape(shape)
    grad_qkv = jnp.concatenate([column(1), column(2), column(3)], axis=1)
    grad_normed = dot_last(grad_qkv, qkv_space_ref[...])
    normed, inverse = norm_stats(hidden)
    cotangent = both_ref[:, 1].reshape(tokens, features).astype(F32)
    grad_hidden = (
        cotangent + norm_backward(grad_normed, gain_space_ref[...], normed, inverse)
    ).astype(BF16)
    grad_out = dot_last(grad_hidden, out_time_ref[...]).astype(BF16)
    qkv = qkv_ref[...]
    keys_t = qkv[:, features : 2 * features].T
    grad_out_t = grad_out.T
    product_t = (grad_out.astype(F32) * attended_ref[...].astype(F32)).T
    queries_t = qkv[:, :features].T

    def attention(h):
        own = slice(h * size, (h + 1) * size)
        delta = jnp.sum(product_t[own], axis=0, keepdims=True)
        weights = weights_ref[h]
        inverse = inverse_ref[h : h + 1]
        values = qkv[:, 2 * features + h * size : 2 * features + (h + 1) * size]
        grad_prob = dot(values, grad_out_t[own])
        yield
        grad_scores = (weights.astype(F32) * (grad_prob - delta)).astype(BF16)
        yield
        queries_grad = dot(keys_t[own], grad_scores) * (inverse * scale)
        keys_grad = dot_last(grad_scores, (queries_t[own].astype(F32) * inverse).astype(BF16))
        values_grad = dot_last(weights, (grad_out_t[own].astype(F32) * inverse).astype(BF16))
        return queries_grad, keys_grad * scale, values_grad

    ended = []
    for h in range(0, HEADS, together):
        ended += in_turn(attention(h + n) for n in range(together))
    queries_grad, keys_grad, values_grad = zip(*ended)
    grad_qkv_time = jnp.concatenate(
        [
            jnp.concatenate(queries_grad, axis=0).T.astype(BF16),
            jnp.concatenate(keys_grad, axis=1).astype(BF16),
            jnp.concatenate(values_grad, axis=1).astype(BF16),
        ],
        axis=1,
    )
    grad_normed_time = dot_last(grad_qkv_time, qkv_time_ref[...])
    tokens_in = both_ref[:, 0].reshape(tokens, features).astype(F32)
    normed_time, inverse_time = norm_stats(tokens_in)
    input_grad = grad_hidden.astype(F32) + norm_backward(
        grad_normed_time, gain_time_ref[...], normed_time, inverse_time
    )
    out_ref[:, 1] = input_grad.astype(BF16).reshape(shape)


def local(
    frame_count, tile_count,
    patch_tokens, gain_time, qkv_time, out_time, gain_space, qkv_space, out_space, cotangent,
):
    frames, patches, features = patch_tokens.shape
    devices = frame_count * tile_count
    own_patches = patches // frame_count
    all_frames = frames * frame_count
    tokens = all_frames * own_patches
    groups = devices // all_frames
    heads = HEADS // groups
    part = features // groups
    params = pltpu.CompilerParams(vmem_limit_bytes=LIMIT)
    def shaped(shape, dtype=BF16):
        return jax.ShapeDtypeStruct(shape, dtype)

    weights = (qkv_time, out_time, qkv_space, out_space)
    far = [pltpu.with_memory_space_constraint(w, pltpu.HBM) for w in weights]
    near = pl.pallas_call(
        fetch_kernel,
        out_shape=(shaped((features, features)),) * 2,
        in_specs=[HBM],
        out_specs=[VMEM] * 2,
        scratch_shapes=[pltpu.SemaphoreType.DMA((2,))],
        compiler_params=pltpu.CompilerParams(vmem_limit_bytes=8 * 1024 * 1024),
        cost_estimate=pl.CostEstimate(flops=0, bytes_accessed=20 * 1024 * 1024, transcendentals=0),
        name="fetch_weights",
    )(far[0])

    both = jnp.stack([patch_tokens, cotangent])
    both = both.reshape(2, frames, frame_count, own_patches, features).transpose(2, 0, 1, 3, 4)
    both = lax.all_to_all(both, "frame", 0, 0)
    both = both.reshape(frame_count, 2, frames * own_patches, features)

    send, hidden, qkv, attended, scores, inverse = pl.pallas_call(
        functools.partial(time_forward_kernel, own_patches, groups, 6),
        out_shape=(
            shaped((groups, tokens, 4 * part)),
            shaped((tokens, features)),
            shaped((tokens, 3 * features)),
            shaped((tokens, features)),
            shaped((HEADS, tokens, tokens)),
            shaped((HEADS, tokens), F32),
        ),
        in_specs=[VMEM] * 5 + [HBM] * 4,
        out_specs=[VMEM] * 6,
        scratch_shapes=[
            pltpu.VMEM((features, features), BF16),
            pltpu.VMEM((features, features), BF16),
            pltpu.VMEM((features, features), BF16),
            pltpu.VMEM(qkv_space.shape, BF16),
            pltpu.SemaphoreType.DMA((4,)),
        ],
        compiler_params=params,
        name="time_forward",
    )(both, gain_time, gain_space, *near, *far)

    got = lax.all_to_all(
        send.reshape(devices, own_patches, 4 * part), ("frame", "tile"), 0, 0
    ).reshape(devices * own_patches, 4 * part)

    rows = devices * own_patches
    size = features // HEADS
    back = pl.pallas_call(
        functools.partial(space_kernel, heads, 256, 4),
        out_shape=shaped((rows, 4 * part)),
        in_specs=[VMEM],
        out_specs=VMEM,
        scratch_shapes=[
            pltpu.VMEM((2, heads, rows, size), BF16),
            pltpu.VMEM((4, heads, size + 16, rows), BF16),
            pltpu.VMEM((heads, size, rows), BF16),
            pltpu.VMEM((heads, size, rows), BF16),
            pltpu.VMEM((heads, rows, size), F32),
            pltpu.VMEM((heads, rows, size), F32),
        ],
        compiler_params=params,
        name="space_attention",
    )(got)

    back = lax.all_to_all(
        back.reshape(devices, own_patches, 4 * part), ("frame", "tile"), 0, 0
    ).reshape(groups, tokens, 4 * part)

    result = pl.pallas_call(
        functools.partial(time_backward_kernel, 6),
        out_shape=shaped(both.shape),
        in_specs=[VMEM] * 13,
        out_specs=VMEM,
        compiler_params=params,
        name="time_backward",
    )(both, back, hidden, qkv, attended, scores, inverse, gain_time, gain_space, *weights)

    result = lax.all_to_all(result, "frame", 0, 0)
    result = result.reshape(frame_count, 2, frames, own_patches, features).transpose(1, 2, 0, 3, 4)
    result = result.reshape(2, frames, patches, features)
    return result[0], result[1]


def solution(mesh):
    in_specs = (P("frame", "tile", None), P(), P(), P(), P(), P(), P(), P("frame", "tile", None))
    out_specs = (P("frame", "tile", None), P("frame", "tile", None))
    return jax.shard_map(
        functools.partial(local, mesh.shape["frame"], mesh.shape["tile"]),
        mesh=mesh, in_specs=in_specs, out_specs=out_specs, check_vma=False,
    )
```

```python
import functools

import jax
import jax.numpy as jnp
from jax import lax
from jax.experimental import pallas as pl
from jax.experimental.pallas import tpu as pltpu
from jax.sharding import PartitionSpec as P

HEADS = 12
EPSILON = 1e-05
F32 = jnp.float32
BF16 = jnp.bfloat16
VMEM = pl.BlockSpec(memory_space=pltpu.VMEM)
HBM = pl.BlockSpec(memory_space=pltpu.HBM)
LIMIT = 32 * 1024 * 1024


def dot(a, b):
    return jnp.dot(a, b, preferred_element_type=F32)


def dot_last(a, b):
    return lax.dot_general(a, b, (((1,), (1,)), ((), ())), preferred_element_type=F32)


def norm_stats(wide):
    average = jnp.mean(wide, axis=-1, keepdims=True)
    centred = wide - average
    inverse = lax.rsqrt(jnp.mean(centred * centred, axis=-1, keepdims=True) + EPSILON)
    return centred * inverse, inverse


def norm_backward(grad_normed, gain, normed, inverse):
    scaled = grad_normed * gain
    return inverse * (
        scaled
        - jnp.mean(scaled, axis=-1, keepdims=True)
        - normed * jnp.mean(scaled * normed, axis=-1, keepdims=True)
    )


def in_turn(running):
    running, ended = list(running), {}
    while len(ended) < len(running):
        for n, one in enumerate(running):
            if n not in ended:
                try:
                    next(one)
                except StopIteration as stop:
                    ended[n] = stop.value
    return [ended[n] for n in range(len(running))]


def fetch_kernel(qkv_hbm, query_ref, key_ref, sems):
    depth = qkv_hbm.shape[0]
    copies = [
        pltpu.make_async_copy(qkv_hbm.at[:, pl.ds(n * depth, depth)], ref, sems.at[n])
        for n, ref in enumerate((query_ref, key_ref))
    ]
    for copy in copies:
        copy.start()
    for copy in copies:
        copy.wait()


def time_forward_kernel(
    patches, groups, together,
    both_ref, gain_time_ref, gain_space_ref, query_time_ref, key_time_ref,
    qkv_time_hbm, out_time_hbm, qkv_space_hbm, out_space_hbm,
    send_ref, hidden_ref, qkv_ref, attended_ref, weights_ref, inverse_ref,
    value_time_ref, out_space_ref, out_time_ref, qkv_space_ref, sems,
):
    depth = qkv_time_hbm.shape[0]
    copies = [
        pltpu.make_async_copy(src, dst, sems.at[n])
        for n, (src, dst) in enumerate((
            (qkv_time_hbm.at[:, pl.ds(2 * depth, depth)], value_time_ref),
            (out_space_hbm, out_space_ref),
            (out_time_hbm, out_time_ref),
            (qkv_space_hbm, qkv_space_ref),
        ))
    ]
    for copy in copies:
        copy.start()
    tokens, features = hidden_ref.shape
    size = features // HEADS
    part = features // groups
    tokens_in = both_ref[:, 0].reshape(tokens, features).astype(F32)
    cotangent = both_ref[:, 1].reshape(tokens, features)
    normed, _ = norm_stats(tokens_in)
    normed_half = (normed * gain_time_ref[...]).astype(BF16)
    queries = dot(normed_half, query_time_ref[...]).astype(BF16)
    keys = dot(normed_half, key_time_ref[...]).astype(BF16)
    qkv_ref[:, :features] = queries
    qkv_ref[:, features : 2 * features] = keys
    queries_t = queries.T * jnp.asarray(size ** -0.5, BF16)
    rows = lax.broadcasted_iota(jnp.int32, (tokens, tokens), 0)
    columns = lax.broadcasted_iota(jnp.int32, (tokens, tokens), 1)
    bias = jnp.where((rows % patches) == (columns % patches), 0.0, -1e30)
    ones = jnp.ones((16, tokens), BF16)

    def attention(h):
        own = slice(h * size, (h + 1) * size)
        scores = dot(keys[:, own], queries_t[own]) + bias
        yield
        weights = jnp.exp(scores - jnp.max(scores, axis=0, keepdims=True)).astype(BF16)
        weights_ref[h] = weights
        yield
        sums = dot(jnp.concatenate([values_t[own], ones], axis=0), weights)
        inverse = 1.0 / sums[size : size + 1]
        inverse_ref[h : h + 1] = inverse
        return (sums[:size] * inverse).astype(BF16)

    first = [attention(h) for h in range(together)]
    for one in first:
        next(one)
    copies[0].wait()
    copies[1].wait()
    values = dot(normed_half, value_time_ref[...]).astype(BF16)
    qkv_ref[:, 2 * features :] = values
    values_t = values.T
    grad_out = dot_last(out_space_ref[...], cotangent).astype(BF16).T
    outputs = in_turn(first)
    for h in range(together, HEADS, together):
        outputs += in_turn(attention(h + n) for n in range(together))
    attended = jnp.concatenate(outputs, axis=0).T
    attended_ref[...] = attended
    copies[2].wait()
    hidden = (tokens_in + dot(attended, out_time_ref[...])).astype(BF16)
    hidden_ref[...] = hidden
    normed_space, _ = norm_stats(hidden.astype(F32))
    space_half = (normed_space * gain_space_ref[...]).astype(BF16)
    copies[3].wait()
    space = dot(space_half, qkv_space_ref[...]).astype(BF16)
    for g in range(groups):
        send_ref[g] = jnp.concatenate(
            [space[:, n * features + g * part : n * features + (g + 1) * part] for n in range(3)]
            + [grad_out[:, g * part : (g + 1) * part]],
            axis=1,
        )


def space_kernel(
    heads, block, together, got_ref, back_ref, nat, tra, out_t, grad_t, grad_key, grad_value
):
    tokens, width = got_ref.shape
    part = width // 4
    size = part // heads
    scale = size ** -0.5
    got = got_ref[...]
    got_t = got.T
    for n in range(4):
        for h in range(heads):
            at = n * part + h * size
            if n in (1, 2):
                nat[n - 1, h] = got[:, at : at + size]
            piece = got_t[at : at + size]
            tra[n, h, :size] = piece * jnp.asarray(scale, BF16) if n == 0 else piece
            if n == 2:
                tra[n, h, size:] = jnp.ones((tra.shape[2] - size, tokens), BF16)
    blocks = tokens // block

    def attention(t):
        h = t // blocks
        here = pl.ds(t % blocks * block, block)
        query_t = tra[0, h, :size, here]
        grad_out_t = tra[3, h, :size, here]
        scores = dot(nat[0, h], query_t)
        yield
        weights = jnp.exp(scores - jnp.max(scores, axis=0, keepdims=True)).astype(BF16)
        yield
        sums = dot(tra[2, h], weights)
        inverse = 1.0 / sums[size : size + 1]
        attended_t = (sums[:size] * inverse).astype(BF16)
        out_t[h, :, here] = attended_t
        delta = jnp.sum(grad_out_t.astype(F32) * attended_t.astype(F32), axis=0, keepdims=True)
        grad_prob = dot(nat[1, h], grad_out_t)
        grad_scores = (weights.astype(F32) * (grad_prob - delta)).astype(BF16)
        yield
        grad_t[h, :, here] = (dot(tra[1, h, :size], grad_scores) * (inverse * scale)).astype(BF16)
        key_terms = dot_last(grad_scores, (query_t.astype(F32) * inverse).astype(BF16))
        value_terms = dot_last(weights, (grad_out_t.astype(F32) * inverse).astype(BF16))
        if t % blocks == 0:
            grad_key[h], grad_value[h] = key_terms, value_terms
        else:
            grad_key[h] += key_terms
            grad_value[h] += value_terms

    for t in range(0, heads * blocks, together):
        in_turn(attention(t + n) for n in range(together))
    back_ref[:, : part * 2] = jnp.concatenate(
        [out_t[h] for h in range(heads)] + [grad_t[h] for h in range(heads)], axis=0
    ).T
    back_ref[:, part * 2 :] = jnp.concatenate(
        [grad_key[h] for h in range(heads)] + [grad_value[h] for h in range(heads)], axis=1
    ).astype(BF16)


def time_backward_kernel(
    together,
    both_ref, back_ref, hidden_ref, qkv_ref, attended_ref, weights_ref, inverse_ref, gain_time_ref, gain_space_ref,
    qkv_time_ref, out_time_ref, qkv_space_ref, out_space_ref, out_ref,
):
    tokens, features = hidden_ref.shape
    groups = back_ref.shape[0]
    part = features // groups
    size = features // HEADS
    scale = size ** -0.5
    shape = (both_ref.shape[0],) + both_ref.shape[2:]

    def column(n):
        return jnp.concatenate(
            [back_ref[g, :, n * part : (n + 1) * part] for g in range(groups)], axis=1
        )

    hidden = hidden_ref[...].astype(F32)
    block_output = (hidden + dot(column(0), out_space_ref[...])).astype(BF16)
    out_ref[:, 0] = block_output.reshape(shape)
    grad_qkv = jnp.concatenate([column(1), column(2), column(3)], axis=1)
    grad_normed = dot_last(grad_qkv, qkv_space_ref[...])
    normed, inverse = norm_stats(hidden)
    cotangent = both_ref[:, 1].reshape(tokens, features).astype(F32)
    grad_hidden = (
        cotangent + norm_backward(grad_normed, gain_space_ref[...], normed, inverse)
    ).astype(BF16)
    grad_out_t = dot_last(out_time_ref[...], grad_hidden).astype(BF16)
    qkv = qkv_ref[...]
    keys_t = qkv[:, features : 2 * features].T
    product_t = grad_out_t.astype(F32) * attended_ref[...].T.astype(F32)
    queries_t = qkv[:, :features].T

    def attention(h):
        own = slice(h * size, (h + 1) * size)
        delta = jnp.sum(product_t[own], axis=0, keepdims=True)
        weights = weights_ref[h]
        inverse = inverse_ref[h : h + 1]
        values = qkv[:, 2 * features + h * size : 2 * features + (h + 1) * size]
        grad_prob = dot(values, grad_out_t[own])
        yield
        grad_scores = (weights.astype(F32) * (grad_prob - delta)).astype(BF16)
        yield
        queries_grad = dot(keys_t[own], grad_scores) * (inverse * scale)
        keys_grad = dot_last(grad_scores, (queries_t[own].astype(F32) * inverse).astype(BF16))
        values_grad = dot_last(weights, (grad_out_t[own].astype(F32) * inverse).astype(BF16))
        return queries_grad, keys_grad * scale, values_grad

    ended = []
    for h in range(0, HEADS, together):
        ended += in_turn(attention(h + n) for n in range(together))
    queries_grad, keys_grad, values_grad = zip(*ended)
    grad_qkv_time = jnp.concatenate(
        [
            jnp.concatenate([g.astype(BF16) for g in queries_grad], axis=0).T,
            jnp.concatenate(keys_grad, axis=1).astype(BF16),
            jnp.concatenate(values_grad, axis=1).astype(BF16),
        ],
        axis=1,
    )
    grad_normed_time = dot_last(grad_qkv_time, qkv_time_ref[...])
    tokens_in = both_ref[:, 0].reshape(tokens, features).astype(F32)
    normed_time, inverse_time = norm_stats(tokens_in)
    input_grad = grad_hidden.astype(F32) + norm_backward(
        grad_normed_time, gain_time_ref[...], normed_time, inverse_time
    )
    out_ref[:, 1] = input_grad.astype(BF16).reshape(shape)


def local(
    frame_count, tile_count,
    patch_tokens, gain_time, qkv_time, out_time, gain_space, qkv_space, out_space, cotangent,
):
    frames, patches, features = patch_tokens.shape
    devices = frame_count * tile_count
    own_patches = patches // frame_count
    all_frames = frames * frame_count
    tokens = all_frames * own_patches
    groups = devices // all_frames
    heads = HEADS // groups
    part = features // groups
    params = pltpu.CompilerParams(vmem_limit_bytes=LIMIT)
    def shaped(shape, dtype=BF16):
        return jax.ShapeDtypeStruct(shape, dtype)

    weights = (qkv_time, out_time, qkv_space, out_space)
    far = [pltpu.with_memory_space_constraint(w, pltpu.HBM) for w in weights]
    near = pl.pallas_call(
        fetch_kernel,
        out_shape=(shaped((features, features)),) * 2,
        in_specs=[HBM],
        out_specs=[VMEM] * 2,
        scratch_shapes=[pltpu.SemaphoreType.DMA((2,))],
        compiler_params=pltpu.CompilerParams(vmem_limit_bytes=8 * 1024 * 1024),
        cost_estimate=pl.CostEstimate(flops=0, bytes_accessed=20 * 1024 * 1024, transcendentals=0),
        name="fetch_weights",
    )(far[0])

    both = jnp.stack([patch_tokens, cotangent])
    both = both.reshape(2, frames, frame_count, own_patches, features).transpose(2, 0, 1, 3, 4)
    both = lax.all_to_all(both, "frame", 0, 0)
    both = both.reshape(frame_count, 2, frames * own_patches, features)

    send, hidden, qkv, attended, scores, inverse = pl.pallas_call(
        functools.partial(time_forward_kernel, own_patches, groups, 6),
        out_shape=(
            shaped((groups, tokens, 4 * part)),
            shaped((tokens, features)),
            shaped((tokens, 3 * features)),
            shaped((tokens, features)),
            shaped((HEADS, tokens, tokens)),
            shaped((HEADS, tokens), F32),
        ),
        in_specs=[VMEM] * 5 + [HBM] * 4,
        out_specs=[VMEM] * 6,
        scratch_shapes=[
            pltpu.VMEM((features, features), BF16),
            pltpu.VMEM((features, features), BF16),
            pltpu.VMEM((features, features), BF16),
            pltpu.VMEM(qkv_space.shape, BF16),
            pltpu.SemaphoreType.DMA((4,)),
        ],
        compiler_params=params,
        name="time_forward",
    )(both, gain_time, gain_space, *near, *far)

    got = lax.all_to_all(
        send.reshape(devices, own_patches, 4 * part), ("frame", "tile"), 0, 0
    ).reshape(devices * own_patches, 4 * part)

    rows = devices * own_patches
    size = features // HEADS
    back = pl.pallas_call(
        functools.partial(space_kernel, heads, 256, 4),
        out_shape=shaped((rows, 4 * part)),
        in_specs=[VMEM],
        out_specs=VMEM,
        scratch_shapes=[
            pltpu.VMEM((2, heads, rows, size), BF16),
            pltpu.VMEM((4, heads, size + 16, rows), BF16),
            pltpu.VMEM((heads, size, rows), BF16),
            pltpu.VMEM((heads, size, rows), BF16),
            pltpu.VMEM((heads, rows, size), F32),
            pltpu.VMEM((heads, rows, size), F32),
        ],
        compiler_params=params,
        name="space_attention",
    )(got)

    back = lax.all_to_all(
        back.reshape(devices, own_patches, 4 * part), ("frame", "tile"), 0, 0
    ).reshape(groups, tokens, 4 * part)

    result = pl.pallas_call(
        functools.partial(time_backward_kernel, 6),
        out_shape=shaped(both.shape),
        in_specs=[VMEM] * 13,
        out_specs=VMEM,
        compiler_params=params,
        name="time_backward",
    )(both, back, hidden, qkv, attended, scores, inverse, gain_time, gain_space, *weights)

    result = lax.all_to_all(result, "frame", 0, 0)
    result = result.reshape(frame_count, 2, frames, own_patches, features).transpose(1, 2, 0, 3, 4)
    result = result.reshape(2, frames, patches, features)
    return result[0], result[1]


def solution(mesh):
    in_specs = (P("frame", "tile", None), P(), P(), P(), P(), P(), P(), P("frame", "tile", None))
    out_specs = (P("frame", "tile", None), P("frame", "tile", None))
    return jax.shard_map(
        functools.partial(local, mesh.shape["frame"], mesh.shape["tile"]),
        mesh=mesh, in_specs=in_specs, out_specs=out_specs, check_vma=False,
    )
```

```python
import functools

import jax
import jax.numpy as jnp
from jax import lax
from jax.experimental import pallas as pl
from jax.experimental.pallas import tpu as pltpu
from jax.sharding import PartitionSpec as P

HEADS = 12
EPSILON = 1e-05
F32 = jnp.float32
BF16 = jnp.bfloat16
VMEM = pl.BlockSpec(memory_space=pltpu.VMEM)
HBM = pl.BlockSpec(memory_space=pltpu.HBM)
LIMIT = 32 * 1024 * 1024


def dot(a, b):
    return jnp.dot(a, b, preferred_element_type=F32)


def dot_last(a, b):
    return lax.dot_general(a, b, (((1,), (1,)), ((), ())), preferred_element_type=F32)


def norm_stats(wide):
    average = jnp.mean(wide, axis=-1, keepdims=True)
    centred = wide - average
    inverse = lax.rsqrt(jnp.mean(centred * centred, axis=-1, keepdims=True) + EPSILON)
    return centred * inverse, inverse


def norm_backward(grad_normed, gain, normed, inverse):
    scaled = grad_normed * gain
    return inverse * (
        scaled
        - jnp.mean(scaled, axis=-1, keepdims=True)
        - normed * jnp.mean(scaled * normed, axis=-1, keepdims=True)
    )


def in_turn(running):
    running, ended = list(running), {}
    while len(ended) < len(running):
        for n, one in enumerate(running):
            if n not in ended:
                try:
                    next(one)
                except StopIteration as stop:
                    ended[n] = stop.value
    return [ended[n] for n in range(len(running))]


def fetch_kernel(qkv_hbm, query_ref, key_ref, sems):
    depth = qkv_hbm.shape[0]
    copies = [
        pltpu.make_async_copy(qkv_hbm.at[:, pl.ds(n * depth, depth)], ref, sems.at[n])
        for n, ref in enumerate((query_ref, key_ref))
    ]
    for copy in copies:
        copy.start()
    for copy in copies:
        copy.wait()


def time_forward_kernel(
    patches, groups, together,
    both_ref, gain_time_ref, gain_space_ref, query_time_ref, key_time_ref,
    qkv_time_hbm, out_time_hbm, qkv_space_hbm, out_space_hbm,
    send_ref, hidden_ref, qkv_ref, attended_ref, weights_ref, inverse_ref,
    value_time_ref, out_space_ref, out_time_ref, qkv_space_ref, sems,
):
    depth = qkv_time_hbm.shape[0]
    copies = [
        pltpu.make_async_copy(src, dst, sems.at[n])
        for n, (src, dst) in enumerate((
            (qkv_time_hbm.at[:, pl.ds(2 * depth, depth)], value_time_ref),
            (out_space_hbm, out_space_ref),
            (out_time_hbm, out_time_ref),
            (qkv_space_hbm, qkv_space_ref),
        ))
    ]
    for copy in copies:
        copy.start()
    tokens, features = hidden_ref.shape
    size = features // HEADS
    part = features // groups
    tokens_in = both_ref[:, 0].reshape(tokens, features).astype(F32)
    cotangent = both_ref[:, 1].reshape(tokens, features)
    normed, _ = norm_stats(tokens_in)
    normed_half = (normed * gain_time_ref[...]).astype(BF16)
    queries = dot(normed_half, query_time_ref[...]).astype(BF16)
    keys = dot(normed_half, key_time_ref[...]).astype(BF16)
    qkv_ref[:, :features] = queries
    qkv_ref[:, features : 2 * features] = keys
    queries_t = queries.T * jnp.asarray(size ** -0.5, BF16)
    rows = lax.broadcasted_iota(jnp.int32, (tokens, tokens), 0)
    columns = lax.broadcasted_iota(jnp.int32, (tokens, tokens), 1)
    bias = jnp.where((rows % patches) == (columns % patches), 0.0, -1e30)
    ones = jnp.ones((16, tokens), BF16)

    def attention(h):
        own = slice(h * size, (h + 1) * size)
        scores = dot(keys[:, own], queries_t[own]) + bias
        yield
        weights = jnp.exp(scores - jnp.max(scores, axis=0, keepdims=True)).astype(BF16)
        weights_ref[h] = weights
        yield
        sums = dot(jnp.concatenate([values_t[own], ones], axis=0), weights)
        inverse = 1.0 / sums[size : size + 1]
        inverse_ref[h : h + 1] = inverse
        return (sums[:size] * inverse).astype(BF16)

    first = [attention(h) for h in range(together)]
    for one in first:
        next(one)
    copies[0].wait()
    copies[1].wait()
    values = dot(normed_half, value_time_ref[...]).astype(BF16)
    qkv_ref[:, 2 * features :] = values
    values_t = values.T
    grad_out = dot_last(out_space_ref[...], cotangent).astype(BF16).T
    outputs = in_turn(first)
    for h in range(together, HEADS, together):
        outputs += in_turn(attention(h + n) for n in range(together))
    attended = jnp.concatenate(outputs, axis=0).T
    attended_ref[...] = attended
    copies[2].wait()
    hidden = (tokens_in + dot(attended, out_time_ref[...])).astype(BF16)
    hidden_ref[...] = hidden
    normed_space, _ = norm_stats(hidden.astype(F32))
    space_half = (normed_space * gain_space_ref[...]).astype(BF16)
    copies[3].wait()
    space = dot(space_half, qkv_space_ref[...]).astype(BF16)
    for g in range(groups):
        send_ref[g] = jnp.concatenate(
            [space[:, n * features + g * part : n * features + (g + 1) * part] for n in range(3)]
            + [grad_out[:, g * part : (g + 1) * part]],
            axis=1,
        )


def space_kernel(
    heads, block, together, got_ref, back_ref, nat, tra, out_t, grad_t, grad_key, grad_value
):
    tokens, width = got_ref.shape
    part = width // 4
    size = part // heads
    scale = size ** -0.5
    got = got_ref[...]
    got_t = got.T
    for n in range(4):
        for h in range(heads):
            at = n * part + h * size
            if n in (1, 2):
                nat[n - 1, h] = got[:, at : at + size]
            piece = got_t[at : at + size]
            tra[n, h, :size] = piece * jnp.asarray(scale, BF16) if n == 0 else piece
            if n == 2:
                tra[n, h, size:] = jnp.ones((tra.shape[2] - size, tokens), BF16)
    blocks = tokens // block

    def attention(t):
        h = t // blocks
        here = pl.ds(t % blocks * block, block)
        query_t = tra[0, h, :size, here]
        grad_out_t = tra[3, h, :size, here]
        scores = dot(nat[0, h], query_t)
        yield
        weights = jnp.exp(scores - jnp.max(scores, axis=0, keepdims=True)).astype(BF16)
        yield
        sums = dot(tra[2, h], weights)
        inverse = 1.0 / sums[size : size + 1]
        attended_t = (sums[:size] * inverse).astype(BF16)
        out_t[h, :, here] = attended_t
        delta = jnp.sum(grad_out_t.astype(F32) * attended_t.astype(F32), axis=0, keepdims=True)
        grad_prob = dot(nat[1, h], grad_out_t)
        grad_scores = (weights.astype(F32) * (grad_prob - delta)).astype(BF16)
        yield
        grad_t[h, :, here] = (dot(tra[1, h, :size], grad_scores) * (inverse * scale)).astype(BF16)
        key_terms = dot_last(grad_scores, (query_t.astype(F32) * inverse).astype(BF16))
        value_terms = dot_last(weights, (grad_out_t.astype(F32) * inverse).astype(BF16))
        if t % blocks == 0:
            grad_key[h], grad_value[h] = key_terms, value_terms
        else:
            grad_key[h] += key_terms
            grad_value[h] += value_terms

    for t in range(0, heads * blocks, together):
        in_turn(attention(t + n) for n in range(together))
    back_ref[:, : part * 2] = jnp.concatenate(
        [out_t[h] for h in range(heads)] + [grad_t[h] for h in range(heads)], axis=0
    ).T
    back_ref[:, part * 2 :] = jnp.concatenate(
        [grad_key[h] for h in range(heads)] + [grad_value[h] for h in range(heads)], axis=1
    ).astype(BF16)


def time_backward_kernel(
    together,
    both_ref, back_ref, hidden_ref, qkv_ref, attended_ref, weights_ref, inverse_ref, gain_time_ref, gain_space_ref,
    qkv_time_ref, out_time_ref, qkv_space_ref, out_space_ref, out_ref,
):
    tokens, features = hidden_ref.shape
    groups = back_ref.shape[0]
    part = features // groups
    size = features // HEADS
    scale = size ** -0.5
    shape = (both_ref.shape[0],) + both_ref.shape[2:]

    def column(n):
        return jnp.concatenate(
            [back_ref[g, :, n * part : (n + 1) * part] for g in range(groups)], axis=1
        )

    hidden = hidden_ref[...].astype(F32)
    block_output = (hidden + dot(column(0), out_space_ref[...])).astype(BF16)
    out_ref[:, 0] = block_output.reshape(shape)
    grad_qkv = jnp.concatenate([column(1), column(2), column(3)], axis=1)
    grad_normed = dot_last(grad_qkv, qkv_space_ref[...])
    normed, inverse = norm_stats(hidden)
    cotangent = both_ref[:, 1].reshape(tokens, features).astype(F32)
    grad_hidden = (
        cotangent + norm_backward(grad_normed, gain_space_ref[...], normed, inverse)
    ).astype(BF16)
    grad_out_t = dot_last(out_time_ref[...], grad_hidden).astype(BF16)
    qkv = qkv_ref[...]
    keys_t = qkv[:, features : 2 * features].T
    product_t = grad_out_t.astype(F32) * attended_ref[...].T.astype(F32)
    queries_t = qkv[:, :features].T

    def attention(h):
        own = slice(h * size, (h + 1) * size)
        delta = jnp.sum(product_t[own], axis=0, keepdims=True)
        weights = weights_ref[h]
        inverse = inverse_ref[h : h + 1]
        values = qkv[:, 2 * features + h * size : 2 * features + (h + 1) * size]
        grad_prob = dot(values, grad_out_t[own])
        yield
        grad_scores = (weights.astype(F32) * (grad_prob - delta)).astype(BF16)
        yield
        queries_grad = dot(keys_t[own], grad_scores) * (inverse * scale)
        keys_grad = dot_last(grad_scores, (queries_t[own].astype(F32) * inverse).astype(BF16))
        values_grad = dot_last(weights, (grad_out_t[own].astype(F32) * inverse).astype(BF16))
        return queries_grad, keys_grad * scale, values_grad

    ended = []
    for h in range(0, HEADS, together):
        ended += in_turn(attention(h + n) for n in range(together))
    queries_grad, keys_grad, values_grad = zip(*ended)
    grad_qkv_time = jnp.concatenate(
        [
            jnp.concatenate([g.astype(BF16) for g in queries_grad], axis=0).T,
            jnp.concatenate(keys_grad, axis=1).astype(BF16),
            jnp.concatenate(values_grad, axis=1).astype(BF16),
        ],
        axis=1,
    )
    grad_normed_time = dot_last(grad_qkv_time, qkv_time_ref[...])
    tokens_in = both_ref[:, 0].reshape(tokens, features).astype(F32)
    normed_time, inverse_time = norm_stats(tokens_in)
    input_grad = grad_hidden.astype(F32) + norm_backward(
        grad_normed_time, gain_time_ref[...], normed_time, inverse_time
    )
    out_ref[:, 1] = input_grad.astype(BF16).reshape(shape)


def local(
    frame_count, tile_count,
    patch_tokens, gain_time, qkv_time, out_time, gain_space, qkv_space, out_space, cotangent,
):
    frames, patches, features = patch_tokens.shape
    devices = frame_count * tile_count
    own_patches = patches // frame_count
    all_frames = frames * frame_count
    tokens = all_frames * own_patches
    groups = devices // all_frames
    heads = HEADS // groups
    part = features // groups
    params = pltpu.CompilerParams(vmem_limit_bytes=LIMIT)
    def shaped(shape, dtype=BF16):
        return jax.ShapeDtypeStruct(shape, dtype)

    weights = (qkv_time, out_time, qkv_space, out_space)
    far = [pltpu.with_memory_space_constraint(w, pltpu.HBM) for w in weights]
    near = pl.pallas_call(
        fetch_kernel,
        out_shape=(shaped((features, features)),) * 2,
        in_specs=[HBM],
        out_specs=[VMEM] * 2,
        scratch_shapes=[pltpu.SemaphoreType.DMA((2,))],
        compiler_params=pltpu.CompilerParams(vmem_limit_bytes=8 * 1024 * 1024),
        cost_estimate=pl.CostEstimate(flops=0, bytes_accessed=20 * 1024 * 1024, transcendentals=0),
        name="fetch_weights",
    )(far[0])

    both = jnp.stack([patch_tokens, cotangent])
    both = both.reshape(2, frames, frame_count, own_patches, features).transpose(2, 0, 1, 3, 4)
    both = lax.all_to_all(both, "frame", 0, 0)
    both = both.reshape(frame_count, 2, frames * own_patches, features)

    send, hidden, qkv, attended, scores, inverse = pl.pallas_call(
        functools.partial(time_forward_kernel, own_patches, groups, 12),
        out_shape=(
            shaped((groups, tokens, 4 * part)),
            shaped((tokens, features)),
            shaped((tokens, 3 * features)),
            shaped((tokens, features)),
            shaped((HEADS, tokens, tokens)),
            shaped((HEADS, tokens), F32),
        ),
        in_specs=[VMEM] * 5 + [HBM] * 4,
        out_specs=[VMEM] * 6,
        scratch_shapes=[
            pltpu.VMEM((features, features), BF16),
            pltpu.VMEM((features, features), BF16),
            pltpu.VMEM((features, features), BF16),
            pltpu.VMEM(qkv_space.shape, BF16),
            pltpu.SemaphoreType.DMA((4,)),
        ],
        compiler_params=params,
        name="time_forward",
    )(both, gain_time, gain_space, *near, *far)

    got = lax.all_to_all(
        send.reshape(devices, own_patches, 4 * part), ("frame", "tile"), 0, 0
    ).reshape(devices * own_patches, 4 * part)

    rows = devices * own_patches
    size = features // HEADS
    back = pl.pallas_call(
        functools.partial(space_kernel, heads, 256, 4),
        out_shape=shaped((rows, 4 * part)),
        in_specs=[VMEM],
        out_specs=VMEM,
        scratch_shapes=[
            pltpu.VMEM((2, heads, rows, size), BF16),
            pltpu.VMEM((4, heads, size + 16, rows), BF16),
            pltpu.VMEM((heads, size, rows), BF16),
            pltpu.VMEM((heads, size, rows), BF16),
            pltpu.VMEM((heads, rows, size), F32),
            pltpu.VMEM((heads, rows, size), F32),
        ],
        compiler_params=params,
        name="space_attention",
    )(got)

    back = lax.all_to_all(
        back.reshape(devices, own_patches, 4 * part), ("frame", "tile"), 0, 0
    ).reshape(groups, tokens, 4 * part)

    result = pl.pallas_call(
        functools.partial(time_backward_kernel, 6),
        out_shape=shaped(both.shape),
        in_specs=[VMEM] * 13,
        out_specs=VMEM,
        compiler_params=params,
        name="time_backward",
    )(both, back, hidden, qkv, attended, scores, inverse, gain_time, gain_space, *weights)

    result = lax.all_to_all(result, "frame", 0, 0)
    result = result.reshape(frame_count, 2, frames, own_patches, features).transpose(1, 2, 0, 3, 4)
    result = result.reshape(2, frames, patches, features)
    return result[0], result[1]


def solution(mesh):
    in_specs = (P("frame", "tile", None), P(), P(), P(), P(), P(), P(), P("frame", "tile", None))
    out_specs = (P("frame", "tile", None), P("frame", "tile", None))
    return jax.shard_map(
        functools.partial(local, mesh.shape["frame"], mesh.shape["tile"]),
        mesh=mesh, in_specs=in_specs, out_specs=out_specs, check_vma=False,
    )
```
